32 devices in a mesh: tm: 8 (over y, x, core), row: 4 (over z).
Axes of the slice: x: 2, y: 2, z: 4, core: 2. Of those that a mesh axis runs over, the one named last changes fastest.
Arguments:
- frames_in: bfloat16 [16, 16, 64, 256], P('tm', 'row'), may hold values from -6 to 6
- cotangent: bfloat16 [16, 16, 64, 256], P('tm', 'row'), may hold values from -6 to 6
- kernel: bfloat16 [9, 256, 256], replicated, may hold values from -0.125 to 0.125
- readout: bfloat16 [256, 256], replicated, may hold values from -0.375 to 0.375
- feedthrough: float32 [256], replicated, may hold values from 0.5 to 1.5
- decay_rate: float32 [16, 256], P('tm'), may hold values from 0.05 to 1, as said below
- start_state: float32 [16, 64, 256], P('row'), may hold values from -6 to 6
Outputs:
- grad_frames: bfloat16 [16, 16, 64, 256], P('tm', 'row')
- grad_kernel: float32 [9, 256, 256], P(None, 'row')
- grad_readout: float32 [256, 256], P(None, 'row')
The draws below stay inside these ranges and needn't reach their ends.
Inputs may be any that keep to these rules, and one draw needn't show every extreme that they name: `decay_rate`: every entry lies strictly between 0 and 1.
All inputs are finite; a program needn't handle non-finite values.
Results may differ from the reference program's by a relative error of at most 0.015.
Values may be sent and summed in bfloat16 or wider, within the bound.
A program may use at most 64 MiB of HBM per device.

```python
import math
import jax
import jax.numpy as jnp
from jax import lax

C = 256
P_SIZE = 256
WIDTH = 64
WINDOW_FRAMES = 16
HEIGHT = 16


def draw_decay_rate(key, part):
    key_slow = jax.random.fold_in(key, 11)
    key_pace = jax.random.fold_in(key, 12)
    key_quick = jax.random.fold_in(key, 13)
    key_jitter = jax.random.fold_in(key, 14)
    key_place = jax.random.fold_in(key, 15)
    key_depth = jax.random.fold_in(key, 16)
    slow_share = 0.5
    slow_mask = jax.random.bernoulli(key_slow, slow_share, (P_SIZE,))
    slow_pace = jnp.exp(jax.random.uniform(key_pace, (P_SIZE,), jnp.float32, math.log(0.1), math.log(1.0))) / WINDOW_FRAMES
    quick_pace = jnp.exp(jax.random.uniform(key_quick, (P_SIZE,), jnp.float32, math.log(0.125), math.log(0.34)))
    baseline_speed = jnp.where(slow_mask, slow_pace, quick_pace)
    random_wobble = jnp.exp(jax.random.uniform(key_jitter, (WINDOW_FRAMES, P_SIZE), jnp.float32, -0.7, 0.7))
    positions = jax.random.randint(key_place, (3,), 0, WINDOW_FRAMES)
    sudden_spike = jnp.any(jnp.arange(WINDOW_FRAMES)[:, None] == positions[None, :], axis=1)
    stack_depth = jax.random.uniform(key_depth, (WINDOW_FRAMES, 1), jnp.float32, 0.6, 0.85)
    final_output = jnp.exp(-baseline_speed[None, :] * random_wobble) * jnp.where(sudden_spike[:, None], stack_depth, 1.0)
    return final_output.astype(jnp.float32)


def spiked(entries, key, source, target, blocks, factor):
    def block_of(position):
        return (jnp.arange(entries.shape[position]) // (entries.shape[position] // blocks)).reshape((-1,) + (1,) * (entries.ndim - 1 - position))

    one_side = jax.random.permutation(key, blocks)[block_of(target)]
    other_side = (block_of(target) + blocks // 2) % blocks
    return jnp.where((block_of(source) == one_side) | (block_of(source) == other_side), factor * entries, entries)


def shard_levels(rng, shape, split, low, top_value):
    def one(position, shards_of):
        steps = jax.random.uniform(jax.random.fold_in(jax.random.fold_in(rng, 6), position), (shards_of,), jnp.float32, low / len(split), top_value / len(split))
        return jnp.repeat(jnp.exp(steps), shape[position] // shards_of).reshape((-1,) + (1,) * (len(shape) - position - 1))

    factor_of = one(*split[0])
    for cut in split[1:]:
        factor_of = factor_of * one(*cut)
    return factor_of


def centred(stream_key, dims, width, most, cuts=(), dtype=jnp.bfloat16):
    entries = width * jax.random.normal(stream_key, dims, jnp.float32)
    if cuts:
        entries = entries * shard_levels(stream_key, dims, cuts, -0.22, 0.18)
    return jnp.clip(entries, -most, most).astype(dtype)


def gaussian_with(stream_key, dims, scale, limit, split, heavy, kind=jnp.bfloat16):
    result = scale * jax.random.normal(stream_key, dims, jnp.float32)
    if split:
        result = result * shard_levels(stream_key, dims, split, -0.22, 0.18)
    return jnp.clip(spiked(result, jax.random.fold_in(stream_key, 3), *heavy), -limit, limit).astype(kind)


def setup_inputs(seed: int = 0) -> dict:
    keys = jax.random.split(jax.random.key(seed), 8)
    return {
        "frames_in": gaussian_with(keys[0], (WINDOW_FRAMES, HEIGHT, WIDTH, C), 1.0, 6.0, ((0, 8), (1, 4)), (1, 3, 4, 2.0)),
        "cotangent": centred(keys[1], (WINDOW_FRAMES, HEIGHT, WIDTH, C), 1.0, 6.0, ((0, 8), (1, 4))),
        "kernel": centred(keys[2], (9, C, P_SIZE), (9 * C) ** -0.5, 0.125),
        "readout": centred(keys[3], (P_SIZE, C), P_SIZE ** -0.5, 0.375),
        "feedthrough": jnp.clip(jax.random.uniform(keys[4], (C,), jnp.float32, 0.5, 1.5), 0.5, 1.5),
        "decay_rate": draw_decay_rate(jax.random.fold_in(keys[7], 71), 0),
        "start_state": centred(keys[6], (HEIGHT, WIDTH, P_SIZE), 1.0, 6.0, ((0, 4),), jnp.float32),
    }


SQRT_TWO_PI = 0.7978845608
CUBIC = 0.044715

def gelu_slope(mixture):
    inside = SQRT_TWO_PI * (mixture + CUBIC * mixture * mixture * mixture)
    tangent = jnp.tanh(inside)
    return 0.5 * (1.0 + tangent) + 0.5 * mixture * (1.0 - tangent * tangent) * SQRT_TWO_PI * (1.0 + 3.0 * CUBIC * mixture * mixture)

def frame_taps(padded, height, grid_width, flipped):
    pieces = []
    for vertical in range(3):
        for lateral in range(3):
            from_top = 2 - vertical if flipped else vertical
            from_left = 2 - lateral if flipped else lateral
            pieces.append(padded[from_top:from_top + height, from_left:from_left + grid_width, :])
    return jnp.stack(pieces, axis=2).reshape(height * grid_width, 9 * padded.shape[2])

def reference(frames_in, cotangent, kernel, readout, feedthrough, decay_rate, start_state):
    frame_total, height, grid_width, channels = frames_in.shape
    state_width = kernel.shape[2]
    points = height * grid_width
    forward_mat = kernel.reshape(9 * channels, state_width)
    backward_mat = jnp.transpose(kernel, (0, 2, 1)).reshape(9 * state_width, channels)
    gain_all = jnp.sqrt(1.0 - decay_rate * decay_rate)

    def advance(carried, inputs):
        frame_in, rate_now, gain_now = inputs
        padded = jnp.pad(frame_in, ((1, 1), (1, 1), (0, 0)))
        driven = jnp.dot(frame_taps(padded, height, grid_width, False), forward_mat, preferred_element_type=jnp.float32)
        carried = rate_now * carried + gain_now * driven.reshape(height, grid_width, state_width)
        return (carried, carried.astype(jnp.bfloat16))
    _, stored = lax.scan(advance, start_state, (frames_in, decay_rate, gain_all))
    later_rate = jnp.concatenate([decay_rate[1:], jnp.ones((1, state_width), jnp.float32)], axis=0)

    def retreat(carried, inputs):
        adjoint_next, kernel_sum, readout_sum = carried
        frame_in, upstream, states_bf, rate_next, gain_now = inputs
        flat_states = states_bf.reshape(points, state_width)
        mixture = jnp.dot(flat_states, readout, preferred_element_type=jnp.float32)
        slope_bf = (upstream.reshape(points, channels).astype(jnp.float32) * gelu_slope(mixture)).astype(jnp.bfloat16)
        pulled = jnp.dot(slope_bf, readout.T, preferred_element_type=jnp.float32)
        adjoint = pulled.reshape(height, grid_width, state_width) + rate_next * adjoint_next
        grad_drive = (gain_now * adjoint).astype(jnp.bfloat16)
        padded_drive = jnp.pad(grad_drive, ((1, 1), (1, 1), (0, 0)))
        spread = jnp.dot(frame_taps(padded_drive, height, grid_width, True), backward_mat, preferred_element_type=jnp.float32)
        grad_frame = (spread.reshape(height, grid_width, channels) + feedthrough * upstream.astype(jnp.float32)).astype(jnp.bfloat16)
        input_taps = frame_taps(jnp.pad(frame_in, ((1, 1), (1, 1), (0, 0))), height, grid_width, False)
        kernel_sum = kernel_sum + jnp.dot(input_taps.T, grad_drive.reshape(points, state_width), preferred_element_type=jnp.float32)
        readout_sum = readout_sum + jnp.dot(flat_states.T, slope_bf, preferred_element_type=jnp.float32)
        return ((adjoint, kernel_sum, readout_sum), grad_frame)
    initial = (jnp.zeros((height, grid_width, state_width), jnp.float32), jnp.zeros((9 * channels, state_width), jnp.float32), jnp.zeros((state_width, channels), jnp.float32))
    (_, kernel_sum, readout_sum), grad_frames = lax.scan(retreat, initial, (frames_in, cotangent, stored, later_rate, gain_all), reverse=True)
    scaling = 1.0 / math.sqrt(frame_total * height * grid_width)
    return (grad_frames, (kernel_sum * scaling).reshape(9, channels, state_width), readout_sum * scaling)
```

```python
import functools
import math

import jax
import jax.numpy as jnp
from jax import lax
from jax.experimental import pallas as pl
from jax.experimental.pallas import tpu as pltpu
from jax.sharding import PartitionSpec as P

SQRT_TWO_PI = 0.7978845608
CUBIC = 0.044715
F32 = jnp.float32
BF16 = jnp.bfloat16
MESH = pl.DeviceIdType.MESH


def gelu_slope(mixture):
    square = mixture * mixture
    tangent = jnp.tanh(SQRT_TWO_PI * (mixture + CUBIC * square * mixture))
    return 0.5 * (1.0 + tangent) + 0.5 * mixture * (1.0 - tangent * tangent) * SQRT_TWO_PI * (
        1.0 + 3.0 * CUBIC * square
    )


def place(taps, frame, padded_row, cells, rows, width):
    channels = cells.shape[1]
    wide = cells.astype(F32)
    column = lax.broadcasted_iota(jnp.int32, wide.shape, 0)
    before = jnp.where(column == 0, 0.0, pltpu.roll(wide, 1, 0)).astype(BF16)
    after = jnp.where(column == width - 1, 0.0, pltpu.roll(wide, width - 1, 0)).astype(BF16)
    for j, shifted in enumerate((before, cells, after)):
        for i in range(3):
            h = padded_row - i
            if 0 <= h < rows:
                k = 3 * i + j
                taps[
                    pl.ds((frame * rows + h) * width, width), pl.ds(k * channels, channels)
                ] = shifted


def pieces(start, size, block):
    done = 0
    while done < size:
        at = start + done
        length = min(size - done, block - at % block)
        yield at // block, at % block, done, length
        done += length


def fused(
    dims,
    frames, cotangent, kernel, readout, feedthrough, decay, start_state,
    grad_frames, grad_kernel, grad_readout,
    taps, taps_t, kernel_t, drive_taps,
    halo, drive_halo, own_decay, all_decay,
    cot_send, cot_recv, driven, drv_send, drv_recv,
    states_bf, slopes, pulled, gd_send, gd_recv, drive,
    grads, pair_recv, chip_send, chip_recv, total, row_send, row_recv, final,
    halo_ss, halo_rs, dec_ss, dec_rs, cot_ss, cot_rs, drv_ss, drv_rs, gd_ss, gd_rs,
    dhalo_ss, dhalo_rs, pair_ss, pair_rs, chip_ss, chip_rs, row_ss, row_rs, fin_ss, fin_rs,
):
    n, nz, tap_rows = dims
    frames_here, rows, width, channels = frames.shape
    state_width = kernel.shape[1]
    band_cells = rows * width
    share = band_cells // n
    chips = n // 2
    half = state_width // 2
    me = lax.axis_index("tm")
    band = lax.axis_index("row")
    core = lax.rem(me, 2)
    chip = lax.div(me, 2)

    def remote(src, dst, send_sem, recv_sem, where):
        return pltpu.make_async_remote_copy(
            src_ref=src, dst_ref=dst, send_sem=send_sem, recv_sem=recv_sem,
            device_id=where, device_id_type=MESH,
        )

    barrier = pltpu.get_barrier_semaphore()
    for d in range(1, n):
        pl.semaphore_signal(
            barrier, inc=1, device_id={"tm": lax.rem(me + d, n)}, device_id_type=MESH
        )
    for d in range(1, nz):
        pl.semaphore_signal(
            barrier, inc=1, device_id={"row": lax.rem(band + d, nz)}, device_id_type=MESH
        )

    own_decay[...] = jnp.zeros_like(own_decay)
    own_decay[0:frames_here, :] = decay[...]
    all_decay[me] = own_decay[...]
    for s in range(n):
        cot_send[s] = jnp.concatenate(
            [cotangent[f, s * share : (s + 1) * share, :] for f in range(frames_here)], axis=0
        )
    cot_recv[me] = cot_send[me]
    pl.semaphore_wait(barrier, (n - 1) + (nz - 1))

    def edge_copies(src, dst, ss, rs):
        up = remote(src.at[:, 0], dst.at[1], ss.at[0], rs.at[1], {"row": band - 1})
        down = remote(src.at[:, rows - 1], dst.at[0], ss.at[1], rs.at[0], {"row": band + 1})
        return up, down

    def edge_start(src, dst, ss, rs):
        up, down = edge_copies(src, dst, ss, rs)

        @pl.when(band > 0)
        def _():
            up.start()

        @pl.when(band < nz - 1)
        def _():
            down.start()

        @pl.when(band == 0)
        def _():
            dst[0] = jnp.zeros(dst.shape[1:], BF16)

        @pl.when(band == nz - 1)
        def _():
            dst[1] = jnp.zeros(dst.shape[1:], BF16)

    def edge_wait(src, dst, ss, rs, arrived):
        up, down = edge_copies(src, dst, ss, rs)

        @pl.when(band > 0)
        def _():
            if arrived:
                down.wait_recv()
            else:
                up.wait_send()

        @pl.when(band < nz - 1)
        def _():
            if arrived:
                up.wait_recv()
            else:
                down.wait_send()

    edge_start(frames, halo, halo_ss, halo_rs)

    def over_tm(src_of, dst, ss, rs):
        copies = []
        for d in range(1, n):
            to = lax.rem(me + d, n)
            copies.append(
                remote(src_of(to), dst.at[me], ss.at[d - 1], rs.at[d - 1], {"tm": to})
            )
        return copies

    dec_copies = over_tm(lambda to: own_decay, all_decay, dec_ss, dec_rs)
    cot_copies = over_tm(lambda to: cot_send.at[to], cot_recv, cot_ss, cot_rs)
    for copy in dec_copies + cot_copies:
        copy.start()

    for f in range(frames_here):
        for r in range(rows):
            place(taps, f, r + 1, frames[f, r], rows, width)
    edge_wait(frames, halo, halo_ss, halo_rs, True)
    for f in range(frames_here):
        place(taps, f, 0, halo[0, f], rows, width)
        place(taps, f, rows + 1, halo[1, f], rows, width)
    driven[...] = jnp.dot(taps[...], kernel[...], preferred_element_type=F32)
    for s in range(n):
        drv_send[s] = jnp.concatenate(
            [
                driven[f * band_cells + s * share : f * band_cells + (s + 1) * share, :]
                for f in range(frames_here)
            ],
            axis=0,
        ).astype(BF16)
    drv_copies = over_tm(lambda to: drv_send.at[to], drv_recv, drv_ss, drv_rs)
    for copy in drv_copies:
        copy.start()
    drv_recv[me] = drv_send[me]

    for k in range(9):
        taps_t[pl.ds(k * channels, channels), :] = taps[:, pl.ds(k * channels, channels)].T
        kernel_t[pl.ds(k * state_width, state_width), :] = kernel[
            pl.ds((8 - k) * channels, channels), :
        ].T

    for copy in dec_copies + drv_copies:
        copy.wait_recv()
    state = start_state[pl.ds(pl.multiple_of(me * share, share), share), :]
    for s in range(n):
        arrived = drv_recv[s].astype(F32)
        kept = []
        for f in range(frames_here):
            rate = all_decay[s, f : f + 1, :]
            gain = jnp.sqrt(1.0 - rate * rate)
            state = rate * state + gain * arrived[f * share : (f + 1) * share]
            kept.append(state)
        states_bf[s] = jnp.concatenate(kept, axis=0).astype(BF16)
    for copy in cot_copies:
        copy.wait_recv()
    flat = n * frames_here * share
    flat_states = states_bf[...].reshape(flat, state_width)
    mixture = jnp.dot(flat_states, readout[...], preferred_element_type=F32)
    slopes[...] = (
        cot_recv[...].reshape(flat, channels).astype(F32) * gelu_slope(mixture)
    ).astype(BF16)
    pulled[...] = lax.dot_general(
        slopes[...], readout[...], (((1,), (1,)), ((), ())), preferred_element_type=F32
    )
    adjoint = jnp.zeros((share, state_width), F32)
    rate = jnp.zeros((1, state_width), F32)
    for s in reversed(range(n)):
        kept = []
        for f in reversed(range(frames_here)):
            at = (s * frames_here + f) * share
            adjoint = pulled[at : at + share, :] + rate * adjoint
            rate = all_decay[s, f : f + 1, :]
            kept.append(jnp.sqrt(1.0 - rate * rate) * adjoint)
        gd_send[s] = jnp.concatenate(kept[::-1], axis=0).astype(BF16)
    gd_copies = over_tm(lambda to: gd_send.at[to], gd_recv, gd_ss, gd_rs)
    for copy in gd_copies:
        copy.start()
    gd_recv[me] = gd_send[me]

    rows_here = channels // nz
    block = tap_rows * rows_here // chips

    def keep(k, product):
        rounded = product.astype(BF16)
        for z in range(nz):
            for j, offset, at, length in pieces(k * rows_here, rows_here, block):
                begin = z * rows_here + at
                for h in range(2):
                    grads[h, j, z, pl.ds(offset, length), :] = rounded[
                        begin : begin + length, h * half : (h + 1) * half
                    ]

    keep(
        9,
        lax.dot_general(
            slopes[...], flat_states, (((0,), (0,)), ((), ())), preferred_element_type=F32
        ),
    )
    for k in range(10, tap_rows):
        keep(k, jnp.zeros((channels, state_width), F32))
    for copy in gd_copies:
        copy.wait_recv()
    for f in range(frames_here):
        drive[f] = (
            jnp.concatenate(
                [gd_recv[s, f * share : (f + 1) * share, :].astype(F32) for s in range(n)], axis=0
            )
            .astype(BF16)
            .reshape(rows, width, state_width)
        )
    edge_start(drive, drive_halo, dhalo_ss, dhalo_rs)
    flat_drive = drive[...].reshape(frames_here * band_cells, state_width)
    for k in range(9):
        keep(
            k,
            jnp.dot(
                taps_t[pl.ds(k * channels, channels), :], flat_drive, preferred_element_type=F32
            ),
        )

    pair_copies = []
    for d in list(range(1, chips)) + [0]:
        j = lax.rem(chip + d, chips)
        pair_copies.append(
            remote(
                grads.at[1 - core, j], pair_recv.at[j], pair_ss.at[d], pair_rs.at[d],
                {"tm": me + 1 - 2 * core},
            )
        )
        pair_copies[-1].start()
    for f in range(frames_here):
        for r in range(rows):
            place(drive_taps, f, r + 1, drive[f, r], rows, width)

    chip_copies = []
    for d in range(1, chips):
        j = lax.rem(chip + d, chips)
        pair_copies[d - 1].wait_recv()
        chip_send[d - 1] = (grads[core, j].astype(F32) + pair_recv[j].astype(F32)).astype(BF16)
        chip_copies.append(
            remote(
                chip_send.at[d - 1], chip_recv.at[d - 1], chip_ss.at[d - 1], chip_rs.at[d - 1],
                {"tm": 2 * j + core},
            )
        )
        chip_copies[-1].start()
    pair_copies[-1].wait_recv()
    total[...] = grads[core, chip].astype(F32) + pair_recv[chip].astype(F32)

    edge_wait(drive, drive_halo, dhalo_ss, dhalo_rs, True)
    for f in range(frames_here):
        place(drive_taps, f, 0, drive_halo[0, f], rows, width)
        place(drive_taps, f, rows + 1, drive_halo[1, f], rows, width)
    spread = jnp.dot(drive_taps[...], kernel_t[...], preferred_element_type=F32)
    for f in range(frames_here):
        grad_frames[f] = (
            spread[f * band_cells : (f + 1) * band_cells]
            + feedthrough[...] * cotangent[f].astype(F32)
        ).astype(BF16)

    for copy in chip_copies:
        copy.wait_recv()
    summed = total[...]
    for d in range(1, chips):
        summed = summed + chip_recv[d - 1].astype(F32)
    total[...] = summed
    row_send[...] = summed.astype(BF16)

    row_copies = []
    for d in range(1, nz):
        z = lax.rem(band + d, nz)
        row_copies.append(
            remote(
                row_send.at[z], row_recv.at[d - 1], row_ss.at[d - 1], row_rs.at[d - 1], {"row": z}
            )
        )
        row_copies[-1].start()
    for copy in row_copies:
        copy.wait_recv()
    mine = total[band]
    for d in range(1, nz):
        mine = mine + row_recv[d - 1].astype(F32)
    final[me] = mine.astype(BF16)

    fin_copies = over_tm(lambda to: final.at[me], final, fin_ss, fin_rs)
    for copy in fin_copies:
        copy.start()
    for copies in (dec_copies, cot_copies, drv_copies, gd_copies, pair_copies, chip_copies):
        for copy in copies:
            copy.wait_send()
    edge_wait(frames, halo, halo_ss, halo_rs, False)
    edge_wait(drive, drive_halo, dhalo_ss, dhalo_rs, False)
    for copy in row_copies:
        copy.wait_send()
    for copy in fin_copies:
        copy.wait_recv()
    scaling = 1.0 / math.sqrt(frames_here * band_cells * n * nz)
    for k in range(10):
        for j, offset, at, length in pieces(k * rows_here, rows_here, block):
            for h in range(2):
                value = final[2 * j + h, pl.ds(offset, length), :].astype(F32) * scaling
                lanes = pl.ds(h * half, half)
                if k < 9:
                    grad_kernel[k, pl.ds(at, length), lanes] = value
                else:
                    grad_readout[pl.ds(at, length), lanes] = value
    for copy in fin_copies:
        copy.wait_send()


def local(n, nz, frames_in, cotangent, kernel, readout, feedthrough, decay_rate, start_state):
    frames_here, rows, width, channels = frames_in.shape
    state_width = kernel.shape[2]
    cells = rows * width
    share = cells // n
    chips = n // 2
    rows_here = channels // nz
    half = state_width // 2
    tap_rows = 10
    while tap_rows * rows_here % (16 * chips):
        tap_rows += 1
    block = tap_rows * rows_here // chips
    mixed = frames_here * share
    vmem = pltpu.VMEM
    dma = pltpu.SemaphoreType.DMA
    whole = pl.BlockSpec(memory_space=pltpu.VMEM)
    every = frames_here * cells
    scratch = [
        vmem((every, 9 * channels), BF16),
        vmem((9 * channels, every), BF16),
        vmem((9 * state_width, channels), BF16),
        vmem((every, 9 * state_width), BF16),
        vmem((2, frames_here, width, channels), BF16),
        vmem((2, frames_here, width, state_width), BF16),
        vmem((8, state_width), F32),
        vmem((n, 8, state_width), F32),
        vmem((n, mixed, channels), BF16),
        vmem((n, mixed, channels), BF16),
        vmem((every, state_width), F32),
        vmem((n, mixed, state_width), BF16),
        vmem((n, mixed, state_width), BF16),
        vmem((n, mixed, state_width), BF16),
        vmem((n * mixed, channels), BF16),
        vmem((n * mixed, state_width), F32),
        vmem((n, mixed, state_width), BF16),
        vmem((n, mixed, state_width), BF16),
        vmem((frames_here, rows, width, state_width), BF16),
        vmem((2, chips, nz, block, half), BF16),
        vmem((chips, nz, block, half), BF16),
        vmem((chips - 1, nz, block, half), BF16),
        vmem((chips - 1, nz, block, half), BF16),
        vmem((nz, block, half), F32),
        vmem((nz, block, half), BF16),
        vmem((nz - 1, block, half), BF16),
        vmem((n, block, half), BF16),
    ]
    for count in (2, n - 1, n - 1, n - 1, n - 1, 2, chips, chips - 1, nz - 1, n - 1):
        scratch += [dma((count,)), dma((count,))]
    spread, kernel_part, readout_part = pl.pallas_call(
        functools.partial(fused, (n, nz, tap_rows)),
        out_shape=(
            jax.ShapeDtypeStruct((frames_here, cells, channels), BF16),
            jax.ShapeDtypeStruct((9, rows_here, state_width), F32),
            jax.ShapeDtypeStruct((rows_here, state_width), F32),
        ),
        in_specs=[whole] * 7,
        out_specs=(whole, whole, whole),
        scratch_shapes=scratch,
        compiler_params=pltpu.CompilerParams(
            collective_id=0, has_side_effects=True, vmem_limit_bytes=48 * 1024 * 1024
        ),
        cost_estimate=pl.CostEstimate(
            flops=2 * every * channels * state_width * 30,
            bytes_accessed=6 * 1024 * 1024,
            transcendentals=every * channels,
        ),
        name="conv_s5_backward",
    )(
        frames_in,
        cotangent.reshape(frames_here, cells, channels),
        kernel.reshape(9 * channels, state_width),
        readout,
        feedthrough.reshape(1, channels),
        decay_rate,
        start_state.reshape(cells, state_width),
    )
    return (spread.reshape(frames_in.shape), kernel_part, readout_part.T)


def solution(mesh):
    placed = (
        P("tm", "row", None, None),
        P("tm", "row", None, None),
        P(),
        P(),
        P(),
        P("tm", None),
        P("row", None, None),
    )
    return jax.shard_map(
        functools.partial(local, mesh.shape["tm"], mesh.shape["row"]),
        mesh=mesh,
        in_specs=placed,
        out_specs=(P("tm", "row", None, None), P(None, "row", None), P(None, "row")),
        check_vma=False,
    )
```

```python
import functools
import math

import jax
import jax.numpy as jnp
from jax import lax
from jax.experimental import pallas as pl
from jax.experimental.pallas import tpu as pltpu
from jax.sharding import PartitionSpec as P

SQRT_TWO_PI = 0.7978845608
CUBIC = 0.044715
F32 = jnp.float32
BF16 = jnp.bfloat16
MESH = pl.DeviceIdType.MESH


def gelu_slope(mixture):
    square = mixture * mixture
    tangent = jnp.tanh(SQRT_TWO_PI * (mixture + CUBIC * square * mixture))
    return 0.5 * (1.0 + tangent) + 0.5 * mixture * (1.0 - tangent * tangent) * SQRT_TWO_PI * (
        1.0 + 3.0 * CUBIC * square
    )


def place(taps, frame, padded_row, cells, rows, width):
    channels = cells.shape[1]
    wide = cells.astype(F32)
    column = lax.broadcasted_iota(jnp.int32, wide.shape, 0)
    before = jnp.where(column == 0, 0.0, pltpu.roll(wide, 1, 0)).astype(BF16)
    after = jnp.where(column == width - 1, 0.0, pltpu.roll(wide, width - 1, 0)).astype(BF16)
    for j, shifted in enumerate((before, cells, after)):
        for i in range(3):
            h = padded_row - i
            if 0 <= h < rows:
                k = 3 * i + j
                taps[
                    pl.ds((frame * rows + h) * width, width), pl.ds(k * channels, channels)
                ] = shifted


def pieces(start, size, block):
    done = 0
    while done < size:
        at = start + done
        length = min(size - done, block - at % block)
        yield at // block, at % block, done, length
        done += length


def fused(
    dims,
    frames_hbm, cotangent_hbm, kernel_hbm, readout_hbm, feedthrough_hbm, decay_hbm, start_hbm,
    grad_frames, grad_kernel, grad_readout,
    frames, cotangent, kernel, readout, feedthrough, decay, start_state, load_sems,
    taps, taps_t, kernel_t, drive_taps,
    halo, drive_halo, own_decay, all_decay,
    cot_send, cot_recv, driven, drv_send, drv_recv,
    states_bf, slopes, pulled, gd_send, gd_recv, drive,
    grads_a, grads_b, pair_a, pair_b, send1_a, send1_b, recv1_a, recv1_b, total_a, total_b,
    send2_a, send2_b, recv2_a, recv2_b, final,
    halo_ss, halo_rs, dec_ss, dec_rs, cot_ss, cot_rs, drv_ss, drv_rs, gd_ss, gd_rs,
    dhalo_ss, dhalo_rs, paira_ss, paira_rs, pairb_ss, pairb_rs, one_a_ss, one_a_rs,
    one_b_ss, one_b_rs, two_a_ss, two_a_rs, two_b_ss, two_b_rs, fin_ss, fin_rs,
):
    n, nz, slots_a, slots_b = dims
    loads = [
        pltpu.make_async_copy(src, dst, load_sems.at[i])
        for i, (src, dst) in enumerate(
            (
                (decay_hbm, decay), (frames_hbm, frames), (cotangent_hbm, cotangent),
                (kernel_hbm, kernel), (start_hbm, start_state), (readout_hbm, readout),
                (feedthrough_hbm, feedthrough),
            )
        )
    ]
    for load in loads:
        load.start()
    frames_here, rows, width, channels = frames.shape
    state_width = kernel.shape[1]
    band_cells = rows * width
    share = band_cells // n
    chips = n // 2
    half = state_width // 2
    me = lax.axis_index("tm")
    band = lax.axis_index("row")
    core = lax.rem(me, 2)
    chip = lax.div(me, 2)

    def remote(src, dst, send_sem, recv_sem, where):
        return pltpu.make_async_remote_copy(
            src_ref=src, dst_ref=dst, send_sem=send_sem, recv_sem=recv_sem,
            device_id=where, device_id_type=MESH,
        )

    barrier = pltpu.get_barrier_semaphore()
    for d in range(1, n):
        pl.semaphore_signal(
            barrier, inc=1, device_id={"tm": lax.rem(me + d, n)}, device_id_type=MESH
        )
    for d in range(1, nz):
        pl.semaphore_signal(
            barrier, inc=1, device_id={"row": lax.rem(band + d, nz)}, device_id_type=MESH
        )

    own_decay[...] = jnp.zeros_like(own_decay)
    loads[0].wait()
    own_decay[0:frames_here, :] = decay[...]
    all_decay[me] = own_decay[...]
    pl.semaphore_wait(barrier, (n - 1) + (nz - 1))

    def edge_copies(src, dst, ss, rs):
        up = remote(src.at[:, 0], dst.at[1], ss.at[0], rs.at[1], {"row": band - 1})
        down = remote(src.at[:, rows - 1], dst.at[0], ss.at[1], rs.at[0], {"row": band + 1})
        return up, down

    def edge_start(src, dst, ss, rs):
        up, down = edge_copies(src, dst, ss, rs)

        @pl.when(band > 0)
        def _():
            up.start()

        @pl.when(band < nz - 1)
        def _():
            down.start()

        @pl.when(band == 0)
        def _():
            dst[0] = jnp.zeros(dst.shape[1:], BF16)

        @pl.when(band == nz - 1)
        def _():
            dst[1] = jnp.zeros(dst.shape[1:], BF16)

    def edge_wait(src, dst, ss, rs, arrived):
        up, down = edge_copies(src, dst, ss, rs)

        @pl.when(band > 0)
        def _():
            if arrived:
                down.wait_recv()
            else:
                up.wait_send()

        @pl.when(band < nz - 1)
        def _():
            if arrived:
                up.wait_recv()
            else:
                down.wait_send()

    edge_start(frames_hbm, halo, halo_ss, halo_rs)
    loads[1].wait()
    loads[2].wait()
    for s in range(n):
        cot_send[s] = jnp.concatenate(
            [cotangent[f, s * share : (s + 1) * share, :] for f in range(frames_here)], axis=0
        )
    cot_recv[me] = cot_send[me]

    def over_tm(src_of, dst, ss, rs):
        copies = []
        for d in range(1, n):
            to = lax.rem(me + d, n)
            copies.append(
                remote(src_of(to), dst.at[me], ss.at[d - 1], rs.at[d - 1], {"tm": to})
            )
        return copies

    dec_copies = over_tm(lambda to: own_decay, all_decay, dec_ss, dec_rs)
    cot_copies = over_tm(lambda to: cot_send.at[to], cot_recv, cot_ss, cot_rs)
    for copy in dec_copies + cot_copies:
        copy.start()

    for f in range(frames_here):
        for r in range(rows):
            place(taps, f, r + 1, frames[f, r], rows, width)
    edge_wait(frames_hbm, halo, halo_ss, halo_rs, True)
    for f in range(frames_here):
        place(taps, f, 0, halo[0, f], rows, width)
        place(taps, f, rows + 1, halo[1, f], rows, width)
    loads[3].wait()
    driven[...] = jnp.dot(taps[...], kernel[...], preferred_element_type=F32)
    for s in range(n):
        drv_send[s] = jnp.concatenate(
            [
                driven[f * band_cells + s * share : f * band_cells + (s + 1) * share, :]
                for f in range(frames_here)
            ],
            axis=0,
        ).astype(BF16)
    drv_copies = over_tm(lambda to: drv_send.at[to], drv_recv, drv_ss, drv_rs)
    for copy in drv_copies:
        copy.start()
    drv_recv[me] = drv_send[me]

    for k in range(9):
        taps_t[pl.ds(k * channels, channels), :] = taps[:, pl.ds(k * channels, channels)].T

    for load in loads[4:]:
        load.wait()

    for copy in dec_copies + drv_copies:
        copy.wait_recv()
    state = start_state[pl.ds(pl.multiple_of(me * share, share), share), :]
    for s in range(n):
        arrived = drv_recv[s].astype(F32)
        kept = []
        for f in range(frames_here):
            rate = all_decay[s, f : f + 1, :]
            gain = jnp.sqrt(1.0 - rate * rate)
            state = rate * state + gain * arrived[f * share : (f + 1) * share]
            kept.append(state)
        states_bf[s] = jnp.concatenate(kept, axis=0).astype(BF16)
    for copy in cot_copies:
        copy.wait_recv()
    flat = n * frames_here * share
    flat_states = states_bf[...].reshape(flat, state_width)
    mixture = jnp.dot(flat_states, readout[...], preferred_element_type=F32)
    slopes[...] = (
        cot_recv[...].reshape(flat, channels).astype(F32) * gelu_slope(mixture)
    ).astype(BF16)
    pulled[...] = lax.dot_general(
        slopes[...], readout[...], (((1,), (1,)), ((), ())), preferred_element_type=F32
    )
    adjoint = jnp.zeros((share, state_width), F32)
    rate = jnp.zeros((1, state_width), F32)
    for s in reversed(range(n)):
        kept = []
        for f in reversed(range(frames_here)):
            at = (s * frames_here + f) * share
            adjoint = pulled[at : at + share, :] + rate * adjoint
            rate = all_decay[s, f : f + 1, :]
            kept.append(jnp.sqrt(1.0 - rate * rate) * adjoint)
        gd_send[s] = jnp.concatenate(kept[::-1], axis=0).astype(BF16)
    gd_copies = over_tm(lambda to: gd_send.at[to], gd_recv, gd_ss, gd_rs)
    for copy in gd_copies:
        copy.start()
    gd_recv[me] = gd_send[me]

    rows_here = channels // nz
    block_a = slots_a * rows_here // chips
    block_b = slots_b * rows_here // chips
    taps_a = min(slots_a, 9)
    in_a = {k: i for i, k in enumerate(range(9 - taps_a, 9))}
    in_b = {k: i for i, k in enumerate([9] + [k for k in range(9) if k not in in_a])}

    def keep(k, product):
        rounded = product.astype(BF16)
        part, slot, block = (
            (grads_a, in_a[k], block_a) if k in in_a else (grads_b, in_b[k], block_b)
        )
        for z in range(nz):
            for j, offset, at, length in pieces(slot * rows_here, rows_here, block):
                begin = z * rows_here + at
                place_at = (j, z) if k in in_a else (z, j)
                for h in range(2):
                    part[(h, *place_at, pl.ds(offset, length), slice(None))] = rounded[
                        begin : begin + length, h * half : (h + 1) * half
                    ]

    keep(
        9,
        lax.dot_general(
            slopes[...], flat_states, (((0,), (0,)), ((), ())), preferred_element_type=F32
        ),
    )
    for part, slots, used, block in (
        (grads_a, slots_a, len(in_a), block_a),
        (grads_b, slots_b, len(in_b), block_b),
    ):
        if used < slots:
            for j, offset, _, length in pieces(
                used * rows_here, (slots - used) * rows_here, block
            ):
                for h in range(2):
                    for z in range(nz):
                        place_at = (j, z) if part is grads_a else (z, j)
                        part[(h, *place_at, pl.ds(offset, length), slice(None))] = jnp.zeros(
                            (length, half), BF16
                        )
    for k in range(9):
        kernel_t[pl.ds(k * state_width, state_width), :] = kernel[
            pl.ds((8 - k) * channels, channels), :
        ].T
    for copy in gd_copies:
        copy.wait_recv()
    for f in range(frames_here):
        drive[f] = (
            jnp.concatenate(
                [gd_recv[s, f * share : (f + 1) * share, :].astype(F32) for s in range(n)], axis=0
            )
            .astype(BF16)
            .reshape(rows, width, state_width)
        )
    edge_start(drive, drive_halo, dhalo_ss, dhalo_rs)
    flat_drive = drive[...].reshape(frames_here * band_cells, state_width)
    def tap_gradient(k):
        keep(
            k,
            jnp.dot(
                taps_t[pl.ds(k * channels, channels), :], flat_drive, preferred_element_type=F32
            ),
        )

    def over_pair(grads, pair, own, count, ss, rs):
        copies = []
        for d in list(range(1, count)) + [0]:
            at = lax.rem(own + d, count)
            copies.append(
                remote(
                    grads.at[1 - core, at], pair.at[at], ss.at[d], rs.at[d],
                    {"tm": me + 1 - 2 * core},
                )
            )
            copies[-1].start()
        return copies

    for k in range(9):
        if k in in_b:
            tap_gradient(k)
    pair_b_copies = over_pair(grads_b, pair_b, band, nz, pairb_ss, pairb_rs)
    for k in range(9):
        if k in in_a:
            tap_gradient(k)
    pair_a_copies = over_pair(grads_a, pair_a, chip, chips, paira_ss, paira_rs)

    def first_sum(pair_copies, grads, pair, own, count, send, recv, ss, rs, where, total):
        copies = []
        for d in range(1, count):
            at = lax.rem(own + d, count)
            pair_copies[d - 1].wait_recv()
            send[d - 1] = (grads[core, at].astype(F32) + pair[at].astype(F32)).astype(BF16)
            copies.append(
                remote(send.at[d - 1], recv.at[d - 1], ss.at[d - 1], rs.at[d - 1], where(at))
            )
            copies[-1].start()
        pair_copies[-1].wait_recv()
        total[...] = grads[core, own].astype(F32) + pair[own].astype(F32)
        return copies

    def to_chip(j):
        return {"tm": 2 * j + core}

    def to_band(z):
        return {"row": z}

    one_b = first_sum(
        pair_b_copies, grads_b, pair_b, band, nz, send1_b, recv1_b, one_b_ss, one_b_rs,
        to_band, total_b,
    )
    one_a = first_sum(
        pair_a_copies, grads_a, pair_a, chip, chips, send1_a, recv1_a, one_a_ss, one_a_rs,
        to_chip, total_a,
    )

    for f in range(frames_here):
        for r in range(rows):
            place(drive_taps, f, r + 1, drive[f, r], rows, width)
    edge_wait(drive, drive_halo, dhalo_ss, dhalo_rs, True)
    for f in range(frames_here):
        place(drive_taps, f, 0, drive_halo[0, f], rows, width)
        place(drive_taps, f, rows + 1, drive_halo[1, f], rows, width)
    spread = jnp.dot(drive_taps[...], kernel_t[...], preferred_element_type=F32)
    for f in range(frames_here):
        grad_frames[f] = (
            spread[f * band_cells : (f + 1) * band_cells]
            + feedthrough[...] * cotangent[f].astype(F32)
        ).astype(BF16)

    def second_sum(one, recv1, total, own, count, send, recv, ss, rs, where):
        summed = total[...]
        for i, copy in enumerate(one):
            copy.wait_recv()
            summed = summed + recv1[i].astype(F32)
        total[...] = summed
        send[...] = summed.astype(BF16)
        copies = []
        for d in range(1, count):
            at = lax.rem(own + d, count)
            copies.append(
                remote(send.at[at], recv.at[d - 1], ss.at[d - 1], rs.at[d - 1], where(at))
            )
            copies[-1].start()
        return copies

    two_b = second_sum(
        one_b, recv1_b, total_b, chip, chips, send2_b, recv2_b, two_b_ss, two_b_rs, to_chip
    )
    two_a = second_sum(
        one_a, recv1_a, total_a, band, nz, send2_a, recv2_a, two_a_ss, two_a_rs, to_band
    )
    for two, recv2, total, own, begin, block in (
        (two_b, recv2_b, total_b, chip, block_a, block_b),
        (two_a, recv2_a, total_a, band, 0, block_a),
    ):
        mine = total[own]
        for i, copy in enumerate(two):
            copy.wait_recv()
            mine = mine + recv2[i].astype(F32)
        final[me, pl.ds(begin, block), :] = mine.astype(BF16)

    fin_copies = over_tm(lambda to: final.at[me], final, fin_ss, fin_rs)
    for copy in fin_copies:
        copy.start()
    for copies in (
        dec_copies, cot_copies, drv_copies, gd_copies, pair_a_copies, pair_b_copies, one_a, one_b,
        two_a, two_b,
    ):
        for copy in copies:
            copy.wait_send()
    edge_wait(frames_hbm, halo, halo_ss, halo_rs, False)
    edge_wait(drive, drive_halo, dhalo_ss, dhalo_rs, False)
    for copy in fin_copies:
        copy.wait_recv()
    scaling = 1.0 / math.sqrt(frames_here * band_cells * n * nz)
    for k in range(10):
        slot, block, begin = (
            (in_a[k], block_a, 0) if k in in_a else (in_b[k], block_b, block_a)
        )
        for j, offset, at, length in pieces(slot * rows_here, rows_here, block):
            for h in range(2):
                value = final[2 * j + h, pl.ds(begin + offset, length), :].astype(F32) * scaling
                lanes = pl.ds(h * half, half)
                if k < 9:
                    grad_kernel[k, pl.ds(at, length), lanes] = value
                else:
                    grad_readout[pl.ds(at, length), lanes] = value
    for copy in fin_copies:
        copy.wait_send()


def local(n, nz, frames_in, cotangent, kernel, readout, feedthrough, decay_rate, start_state):
    frames_here, rows, width, channels = frames_in.shape
    state_width = kernel.shape[2]
    cells = rows * width
    share = cells // n
    chips = n // 2
    rows_here = channels // nz
    half = state_width // 2
    step = 16 * chips // math.gcd(rows_here, 16 * chips)
    slots_a = -(-7 // step) * step
    slots_b = -(-max(10 - slots_a, 1) // step) * step
    block_a = slots_a * rows_here // chips
    block_b = slots_b * rows_here // chips
    mixed = frames_here * share
    vmem = pltpu.VMEM
    dma = pltpu.SemaphoreType.DMA
    whole = pl.BlockSpec(memory_space=pltpu.VMEM)
    every = frames_here * cells
    scratch = [
        vmem(frames_in.shape, BF16),
        vmem((frames_here, cells, channels), BF16),
        vmem((9 * channels, state_width), BF16),
        vmem(readout.shape, BF16),
        vmem((1, channels), F32),
        vmem(decay_rate.shape, F32),
        vmem((cells, state_width), F32),
        dma((7,)),
        vmem((every, 9 * channels), BF16),
        vmem((9 * channels, every), BF16),
        vmem((9 * state_width, channels), BF16),
        vmem((every, 9 * state_width), BF16),
        vmem((2, frames_here, width, channels), BF16),
        vmem((2, frames_here, width, state_width), BF16),
        vmem((8, state_width), F32),
        vmem((n, 8, state_width), F32),
        vmem((n, mixed, channels), BF16),
        vmem((n, mixed, channels), BF16),
        vmem((every, state_width), F32),
        vmem((n, mixed, state_width), BF16),
        vmem((n, mixed, state_width), BF16),
        vmem((n, mixed, state_width), BF16),
        vmem((n * mixed, channels), BF16),
        vmem((n * mixed, state_width), F32),
        vmem((n, mixed, state_width), BF16),
        vmem((n, mixed, state_width), BF16),
        vmem((frames_here, rows, width, state_width), BF16),
        vmem((2, chips, nz, block_a, half), BF16),
        vmem((2, nz, chips, block_b, half), BF16),
        vmem((chips, nz, block_a, half), BF16),
        vmem((nz, chips, block_b, half), BF16),
        vmem((chips - 1, nz, block_a, half), BF16),
        vmem((nz - 1, chips, block_b, half), BF16),
        vmem((chips - 1, nz, block_a, half), BF16),
        vmem((nz - 1, chips, block_b, half), BF16),
        vmem((nz, block_a, half), F32),
        vmem((chips, block_b, half), F32),
        vmem((nz, block_a, half), BF16),
        vmem((chips, block_b, half), BF16),
        vmem((nz - 1, block_a, half), BF16),
        vmem((chips - 1, block_b, half), BF16),
        vmem((n, block_a + block_b, half), BF16),
    ]
    counts = (2, n - 1, n - 1, n - 1, n - 1, 2)
    counts += (chips, nz, chips - 1, nz - 1, nz - 1, chips - 1, n - 1)
    for count in counts:
        scratch += [dma((count,)), dma((count,))]
    spread, kernel_part, readout_part = pl.pallas_call(
        functools.partial(fused, (n, nz, slots_a, slots_b)),
        out_shape=(
            jax.ShapeDtypeStruct((frames_here, cells, channels), BF16),
            jax.ShapeDtypeStruct((9, rows_here, state_width), F32),
            jax.ShapeDtypeStruct((rows_here, state_width), F32),
        ),
        in_specs=[pl.BlockSpec(memory_space=pltpu.HBM)] * 7,
        out_specs=(whole, whole, whole),
        scratch_shapes=scratch,
        compiler_params=pltpu.CompilerParams(
            collective_id=0, has_side_effects=True, vmem_limit_bytes=60 * 1024 * 1024
        ),
        cost_estimate=pl.CostEstimate(
            flops=2 * every * channels * state_width * 30,
            bytes_accessed=6 * 1024 * 1024,
            transcendentals=every * channels,
        ),
        name="conv_s5_backward",
    )(
        frames_in,
        cotangent.reshape(frames_here, cells, channels),
        kernel.reshape(9 * channels, state_width),
        readout,
        feedthrough.reshape(1, channels),
        decay_rate,
        start_state.reshape(cells, state_width),
    )
    return (spread.reshape(frames_in.shape), kernel_part, readout_part.T)


def solution(mesh):
    placed = (
        P("tm", "row", None, None),
        P("tm", "row", None, None),
        P(),
        P(),
        P(),
        P("tm", None),
        P("row", None, None),
    )
    return jax.shard_map(
        functools.partial(local, mesh.shape["tm"], mesh.shape["row"]),
        mesh=mesh,
        in_specs=placed,
        out_specs=(P("tm", "row", None, None), P(None, "row", None), P(None, "row")),
        check_vma=False,
    )
```

```python
import functools
import math

import jax
import jax.numpy as jnp
from jax import lax
from jax.experimental import pallas as pl
from jax.experimental.pallas import tpu as pltpu
from jax.sharding import PartitionSpec as P

SQRT_TWO_PI = 0.7978845608
CUBIC = 0.044715
F32 = jnp.float32
BF16 = jnp.bfloat16
MESH = pl.DeviceIdType.MESH


def gelu_slope(mixture):
    square = mixture * mixture
    tangent = jnp.tanh(SQRT_TWO_PI * (mixture + CUBIC * square * mixture))
    return 0.5 * (1.0 + tangent) + 0.5 * mixture * (1.0 - tangent * tangent) * SQRT_TWO_PI * (
        1.0 + 3.0 * CUBIC * square
    )


def place(taps, frame, padded_row, cells, rows, width):
    channels = cells.shape[1]
    wide = cells.astype(F32)
    column = lax.broadcasted_iota(jnp.int32, wide.shape, 0)
    before = jnp.where(column == 0, 0.0, pltpu.roll(wide, 1, 0)).astype(BF16)
    after = jnp.where(column == width - 1, 0.0, pltpu.roll(wide, width - 1, 0)).astype(BF16)
    for j, shifted in enumerate((before, cells, after)):
        for i in range(3):
            h = padded_row - i
            if 0 <= h < rows:
                k = 3 * i + j
                taps[
                    pl.ds((frame * rows + h) * width, width), pl.ds(k * channels, channels)
                ] = shifted


def pieces(start, size, block):
    done = 0
    while done < size:
        at = start + done
        length = min(size - done, block - at % block)
        yield at // block, at % block, done, length
        done += length


def places(slots_a):
    taps_a = min(slots_a, 9)
    in_a = {k: i for i, k in enumerate(range(9 - taps_a, 9))}
    in_b = {k: i for i, k in enumerate([9] + list(range(9 - taps_a)))}
    return in_a, in_b


def fused(
    dims,
    frames_hbm, cotangent_hbm, kernel_hbm, readout_hbm, feedthrough_hbm, decay_hbm, start_hbm,
    grad_frames, gathered,
    frames, cotangent, kernel, readout, feedthrough, decay, start_state, load_sems,
    taps, taps_t, kernel_t, drive_taps,
    halo, drive_halo, own_decay, all_decay,
    cot_send, cot_recv, driven, drv_send, drv_recv,
    states_bf, slopes, pulled, gd_send, gd_recv, drive,
    grads_a, grads_b, pair_a, pair_b, send1_a, send1_b, recv1_a, recv1_b, total_a, total_b,
    send2_a, send2_b, recv2_a, recv2_b, final, spread_bf,
    halo_ss, halo_rs, dec_ss, dec_rs, cot_ss, cot_rs, drv_ss, drv_rs, gd_ss, gd_rs,
    dhalo_ss, dhalo_rs, paira_ss, paira_rs, pairb_ss, pairb_rs, one_a_ss, one_a_rs,
    one_b_ss, one_b_rs, two_a_ss, two_a_rs, two_b_ss, two_b_rs, fin_ss, fin_rs, sib_ss, sib_rs,
):
    n, nz, slots_a, slots_b, groups = dims
    loads = [
        pltpu.make_async_copy(src, dst, load_sems.at[i])
        for i, (src, dst) in enumerate(
            (
                (decay_hbm, decay), (frames_hbm, frames), (cotangent_hbm, cotangent),
                (kernel_hbm, kernel), (start_hbm, start_state), (readout_hbm, readout),
                (feedthrough_hbm, feedthrough),
            )
        )
    ]
    for load in loads:
        load.start()
    frames_here, rows, width, channels = frames.shape
    state_width = kernel.shape[1]
    band_cells = rows * width
    share = band_cells // n
    chips = n // 2
    part_cells = share // groups
    half = state_width // 2
    me = lax.axis_index("tm")
    band = lax.axis_index("row")
    core = lax.rem(me, 2)
    chip = lax.div(me, 2)

    def remote(src, dst, send_sem, recv_sem, where):
        return pltpu.make_async_remote_copy(
            src_ref=src, dst_ref=dst, send_sem=send_sem, recv_sem=recv_sem,
            device_id=where, device_id_type=MESH,
        )

    barrier = pltpu.get_barrier_semaphore()
    for d in range(1, n):
        pl.semaphore_signal(
            barrier, inc=1, device_id={"tm": lax.rem(me + d, n)}, device_id_type=MESH
        )
    for d in range(1, nz):
        pl.semaphore_signal(
            barrier, inc=1, device_id={"row": lax.rem(band + d, nz)}, device_id_type=MESH
        )

    own_decay[...] = jnp.zeros_like(own_decay)
    loads[0].wait()
    own_decay[0:frames_here, :] = decay[...]
    all_decay[me] = own_decay[...]
    pl.semaphore_wait(barrier, (n - 1) + (nz - 1))

    def edge_copies(src, dst, ss, rs):
        up = remote(src.at[:, 0], dst.at[1], ss.at[0], rs.at[1], {"row": band - 1})
        down = remote(src.at[:, rows - 1], dst.at[0], ss.at[1], rs.at[0], {"row": band + 1})
        return up, down

    def edge_start(src, dst, ss, rs):
        up, down = edge_copies(src, dst, ss, rs)

        @pl.when(band > 0)
        def _():
            up.start()

        @pl.when(band < nz - 1)
        def _():
            down.start()

        @pl.when(band == 0)
        def _():
            dst[0] = jnp.zeros(dst.shape[1:], BF16)

        @pl.when(band == nz - 1)
        def _():
            dst[1] = jnp.zeros(dst.shape[1:], BF16)

    def edge_wait(src, dst, ss, rs, arrived):
        up, down = edge_copies(src, dst, ss, rs)

        @pl.when(band > 0)
        def _():
            if arrived:
                down.wait_recv()
            else:
                up.wait_send()

        @pl.when(band < nz - 1)
        def _():
            if arrived:
                up.wait_recv()
            else:
                down.wait_send()

    edge_start(frames_hbm, halo, halo_ss, halo_rs)
    loads[1].wait()
    loads[2].wait()
    def over_tm(src_of, dst, ss, rs):
        copies = []
        for d in range(1, n):
            to = lax.rem(me + d, n)
            copies.append(
                remote(src_of(to), dst.at[me], ss.at[d - 1], rs.at[d - 1], {"tm": to})
            )
        return copies

    def cells_of(s, g):
        begin = s * share + g * part_cells
        return slice(begin, begin + part_cells)

    for g in range(groups):
        for s in range(n):
            cot_send[g, s] = jnp.concatenate(
                [cotangent[f, cells_of(s, g), :] for f in range(frames_here)], axis=0
            )
        cot_recv[g, me] = cot_send[g, me]

    dec_copies = over_tm(lambda to: own_decay, all_decay, dec_ss, dec_rs)
    for copy in dec_copies:
        copy.start()
    cot_copies = []
    for g in range(groups):
        cot_copies.append(
            over_tm(
                lambda to, g=g: cot_send.at[g, to], cot_recv.at[g], cot_ss.at[g], cot_rs.at[g]
            )
        )
        for copy in cot_copies[g]:
            copy.start()

    for f in range(frames_here):
        for r in range(rows):
            place(taps, f, r + 1, frames[f, r], rows, width)
    edge_wait(frames_hbm, halo, halo_ss, halo_rs, True)
    for f in range(frames_here):
        place(taps, f, 0, halo[0, f], rows, width)
        place(taps, f, rows + 1, halo[1, f], rows, width)
    loads[3].wait()
    driven[...] = jnp.dot(taps[...], kernel[...], preferred_element_type=F32).reshape(driven.shape)
    drv_copies = []
    for g in range(groups):
        for s in range(n):
            drv_send[g, s] = jnp.concatenate(
                [driven[f, cells_of(s, g), :] for f in range(frames_here)], axis=0
            ).astype(BF16)
        drv_copies.append(
            over_tm(
                lambda to, g=g: drv_send.at[g, to], drv_recv.at[g], drv_ss.at[g], drv_rs.at[g]
            )
        )
        for copy in drv_copies[g]:
            copy.start()
        drv_recv[g, me] = drv_send[g, me]

    for k in range(9):
        taps_t[pl.ds(k * channels, channels), :] = taps[:, pl.ds(k * channels, channels)].T

    for load in loads[4:7]:
        load.wait()

    for copy in dec_copies:
        copy.wait_recv()
    flat = n * frames_here * part_cells
    gd_copies = []
    for g in range(groups):
        for copy in drv_copies[g]:
            copy.wait_recv()
        begin = pl.multiple_of(me * share + g * part_cells, part_cells)
        state = start_state[pl.ds(begin, part_cells), :]
        for s in range(n):
            arrived = drv_recv[g, s].astype(F32)
            kept = []
            for f in range(frames_here):
                rate = all_decay[s, f : f + 1, :]
                gain = jnp.sqrt(1.0 - rate * rate)
                state = rate * state + gain * arrived[f * part_cells : (f + 1) * part_cells]
                kept.append(state)
            states_bf[g, s] = jnp.concatenate(kept, axis=0).astype(BF16)
        for copy in cot_copies[g]:
            copy.wait_recv()
        mixture = jnp.dot(
            states_bf[g].reshape(flat, state_width), readout[...], preferred_element_type=F32
        )
        slopes[g] = (
            cot_recv[g].reshape(flat, channels).astype(F32) * gelu_slope(mixture)
        ).astype(BF16)
        pulled[...] = lax.dot_general(
            slopes[g], readout[...], (((1,), (1,)), ((), ())), preferred_element_type=F32
        )
        adjoint = jnp.zeros((part_cells, state_width), F32)
        rate = jnp.zeros((1, state_width), F32)
        for s in reversed(range(n)):
            kept = []
            for f in reversed(range(frames_here)):
                at = (s * frames_here + f) * part_cells
                adjoint = pulled[at : at + part_cells, :] + rate * adjoint
                rate = all_decay[s, f : f + 1, :]
                kept.append(jnp.sqrt(1.0 - rate * rate) * adjoint)
            gd_send[g, s] = jnp.concatenate(kept[::-1], axis=0).astype(BF16)
        gd_copies.append(
            over_tm(lambda to, g=g: gd_send.at[g, to], gd_recv.at[g], gd_ss.at[g], gd_rs.at[g])
        )
        for copy in gd_copies[g]:
            copy.start()
        gd_recv[g, me] = gd_send[g, me]

    rows_here = channels // nz
    block_a = slots_a * rows_here // chips
    block_b = slots_b * rows_here // chips
    in_a, in_b = places(slots_a)

    def keep(k, product):
        rounded = product.astype(BF16)
        part, slot, block = (
            (grads_a, in_a[k], block_a) if k in in_a else (grads_b, in_b[k], block_b)
        )
        for z in range(nz):
            for j, offset, at, length in pieces(slot * rows_here, rows_here, block):
                begin = z * rows_here + at
                place_at = (j, z) if k in in_a else (z, j)
                for h in range(2):
                    part[(h, *place_at, pl.ds(offset, length), slice(None))] = rounded[
                        begin : begin + length, h * half : (h + 1) * half
                    ]

    keep(
        9,
        lax.dot_general(
            slopes[...].reshape(groups * flat, channels),
            states_bf[...].reshape(groups * flat, state_width),
            (((0,), (0,)), ((), ())), preferred_element_type=F32
        ),
    )
    for part, slots, used, block in (
        (grads_a, slots_a, len(in_a), block_a),
        (grads_b, slots_b, len(in_b), block_b),
    ):
        if used < slots:
            for j, offset, _, length in pieces(
                used * rows_here, (slots - used) * rows_here, block
            ):
                for h in range(2):
                    for z in range(nz):
                        place_at = (j, z) if part is grads_a else (z, j)
                        part[(h, *place_at, pl.ds(offset, length), slice(None))] = jnp.zeros(
                            (length, half), BF16
                        )
    for k in range(9):
        kernel_t[pl.ds(k * state_width, state_width), :] = kernel[
            pl.ds((8 - k) * channels, channels), :
        ].T
    for copies in gd_copies:
        for copy in copies:
            copy.wait_recv()
    for f in range(frames_here):
        drive[f] = (
            jnp.concatenate(
                [
                    gd_recv[g, s, f * part_cells : (f + 1) * part_cells, :].astype(F32)
                    for s in range(n)
                    for g in range(groups)
                ],
                axis=0,
            )
            .astype(BF16)
            .reshape(rows, width, state_width)
        )
    edge_start(drive, drive_halo, dhalo_ss, dhalo_rs)
    flat_drive = drive[...].reshape(frames_here * band_cells, state_width)
    def tap_gradient(k):
        keep(
            k,
            jnp.dot(
                taps_t[pl.ds(k * channels, channels), :], flat_drive, preferred_element_type=F32
            ),
        )

    def over_pair(grads, pair, own, count, ss, rs):
        copies = []
        for d in list(range(1, count)) + [0]:
            at = lax.rem(own + d, count)
            copies.append(
                remote(
                    grads.at[1 - core, at], pair.at[at], ss.at[d], rs.at[d],
                    {"tm": me + 1 - 2 * core},
                )
            )
            copies[-1].start()
        return copies

    for k in range(9):
        if k in in_b:
            tap_gradient(k)
    pair_b_copies = over_pair(grads_b, pair_b, band, nz, pairb_ss, pairb_rs)
    for k in range(9):
        if k in in_a:
            tap_gradient(k)
    pair_a_copies = over_pair(grads_a, pair_a, chip, chips, paira_ss, paira_rs)

    def first_sum(pair_copies, grads, pair, own, count, send, recv, ss, rs, where, total):
        copies = []
        for d in range(1, count):
            at = lax.rem(own + d, count)
            pair_copies[d - 1].wait_recv()
            send[d - 1] = (grads[core, at].astype(F32) + pair[at].astype(F32)).astype(BF16)
            copies.append(
                remote(send.at[d - 1], recv.at[d - 1], ss.at[d - 1], rs.at[d - 1], where(at))
            )
            copies[-1].start()
        pair_copies[-1].wait_recv()
        total[...] = grads[core, own].astype(F32) + pair[own].astype(F32)
        return copies

    def to_chip(j):
        return {"tm": 2 * j + core}

    def to_band(z):
        return {"row": z}

    one_b = first_sum(
        pair_b_copies, grads_b, pair_b, band, nz, send1_b, recv1_b, one_b_ss, one_b_rs,
        to_band, total_b,
    )
    one_a = first_sum(
        pair_a_copies, grads_a, pair_a, chip, chips, send1_a, recv1_a, one_a_ss, one_a_rs,
        to_chip, total_a,
    )

    for f in range(frames_here):
        for r in range(rows):
            place(drive_taps, f, r + 1, drive[f, r], rows, width)
    edge_wait(drive, drive_halo, dhalo_ss, dhalo_rs, True)
    for f in range(frames_here):
        place(drive_taps, f, 0, drive_halo[0, f], rows, width)
        place(drive_taps, f, rows + 1, drive_halo[1, f], rows, width)
    spread = jnp.dot(drive_taps[...], kernel_t[...], preferred_element_type=F32)
    for f in range(frames_here):
        spread_bf[f] = (
            spread[f * band_cells : (f + 1) * band_cells]
            + feedthrough[...] * cotangent[f].astype(F32)
        ).astype(BF16)

    out_copies = [pltpu.make_async_copy(spread_bf, grad_frames, load_sems.at[7])]
    out_copies[0].start()

    def second_sum(one, recv1, total, own, count, send, recv, ss, rs, where):
        summed = total[...]
        for i, copy in enumerate(one):
            copy.wait_recv()
            summed = summed + recv1[i].astype(F32)
        total[...] = summed
        send[...] = summed.astype(BF16)
        copies = []
        for d in range(1, count):
            at = lax.rem(own + d, count)
            copies.append(
                remote(send.at[at], recv.at[d - 1], ss.at[d - 1], rs.at[d - 1], where(at))
            )
            copies[-1].start()
        return copies

    two_b = second_sum(
        one_b, recv1_b, total_b, chip, chips, send2_b, recv2_b, two_b_ss, two_b_rs, to_chip
    )
    two_a = second_sum(
        one_a, recv1_a, total_a, band, nz, send2_a, recv2_a, two_a_ss, two_a_rs, to_band
    )
    for two, recv2, total, own, begin, block in (
        (two_b, recv2_b, total_b, chip, block_a, block_b),
        (two_a, recv2_a, total_a, band, 0, block_a),
    ):
        mine = total[own]
        for i, copy in enumerate(two):
            copy.wait_recv()
            mine = mine + recv2[i].astype(F32)
        final[me, pl.ds(begin, block), :] = mine.astype(BF16)

    sibling = {"tm": me + 1 - 2 * core}
    fin_copies = []
    for d in range(1, chips):
        j = lax.rem(chip + d, chips)
        fin_copies.append(
            remote(final.at[me], final.at[me], fin_ss.at[d - 1], fin_rs.at[d - 1], to_chip(j))
        )
    sib_copies = []
    for d in range(chips):
        at = 2 * lax.rem(chip - d + chips, chips) + core
        sib_copies.append(
            remote(final.at[at], final.at[at], sib_ss.at[d], sib_rs.at[d], sibling)
        )
    for copy in fin_copies:
        copy.start()
    sib_copies[0].start()
    flat_copies = dec_copies
    for copies in cot_copies + drv_copies + gd_copies:
        flat_copies = flat_copies + copies
    for copies in (pair_a_copies, pair_b_copies, one_a, one_b, two_a, two_b):
        flat_copies = flat_copies + copies
    for copy in flat_copies:
        copy.wait_send()
    edge_wait(frames_hbm, halo, halo_ss, halo_rs, False)
    edge_wait(drive, drive_halo, dhalo_ss, dhalo_rs, False)
    for d in range(1, chips):
        fin_copies[d - 1].wait_recv()
        sib_copies[d].start()
    for copy in sib_copies:
        copy.wait_recv()
    out_copies.append(pltpu.make_async_copy(final, gathered, load_sems.at[8]))
    out_copies[1].start()
    for copy in fin_copies + sib_copies:
        copy.wait_send()
    for copy in out_copies:
        copy.wait()


def finish(
    dims,
    spread, gathered, grad_frames, grad_kernel, grad_readout,
    final, scaled, scaled_readout, sems,
):
    chips, slots_a, block_a, block_b, in_a, in_b, scaling = dims
    rows_here, state_width = scaled_readout.shape
    half = state_width // 2
    through = pltpu.make_async_copy(spread, grad_frames, sems.at[0])
    load = pltpu.make_async_copy(gathered, final, sems.at[1])
    load.start()
    through.start()
    load.wait()
    for k in range(10):
        slot, block, begin = (in_a[k], block_a, 0) if k in in_a else (in_b[k], block_b, block_a)
        for j, offset, at, length in pieces(slot * rows_here, rows_here, block):
            for h in range(2):
                value = final[2 * j + h, pl.ds(begin + offset, length), :].astype(F32) * scaling
                lanes = pl.ds(h * half, half)
                if k < 9:
                    scaled[k, pl.ds(at, length), lanes] = value
                else:
                    scaled_readout[pl.ds(at, length), lanes] = value
    stores = [
        pltpu.make_async_copy(scaled, grad_kernel, sems.at[2]),
        pltpu.make_async_copy(scaled_readout, grad_readout, sems.at[3]),
    ]
    for store in stores:
        store.start()
    for copy in stores + [through]:
        copy.wait()


def local(n, nz, frames_in, cotangent, kernel, readout, feedthrough, decay_rate, start_state):
    frames_here, rows, width, channels = frames_in.shape
    state_width = kernel.shape[2]
    cells = rows * width
    share = cells // n
    chips = n // 2
    rows_here = channels // nz
    half = state_width // 2
    step = 16 * chips // math.gcd(rows_here, 16 * chips)
    slots_a = -(-7 // step) * step
    slots_b = -(-max(10 - slots_a, 1) // step) * step
    block_a = slots_a * rows_here // chips
    block_b = slots_b * rows_here // chips
    groups = 2 if frames_here * share // 2 % 16 == 0 and share % 16 == 0 else 1
    mixed = frames_here * share // groups
    scaling = 1.0 / math.sqrt(frames_here * cells * n * nz)
    vmem = pltpu.VMEM
    dma = pltpu.SemaphoreType.DMA
    any_space = pl.BlockSpec(memory_space=pl.ANY)
    hbm = pl.BlockSpec(memory_space=pltpu.HBM)
    every = frames_here * cells
    scratch = [
        vmem(frames_in.shape, BF16),
        vmem((frames_here, cells, channels), BF16),
        vmem((9 * channels, state_width), BF16),
        vmem(readout.shape, BF16),
        vmem((1, channels), F32),
        vmem(decay_rate.shape, F32),
        vmem((cells, state_width), F32),
        dma((9,)),
        vmem((every, 9 * channels), BF16),
        vmem((9 * channels, every), BF16),
        vmem((9 * state_width, channels), BF16),
        vmem((every, 9 * state_width), BF16),
        vmem((2, frames_here, width, channels), BF16),
        vmem((2, frames_here, width, state_width), BF16),
        vmem((8, state_width), F32),
        vmem((n, 8, state_width), F32),
        vmem((groups, n, mixed, channels), BF16),
        vmem((groups, n, mixed, channels), BF16),
        vmem((frames_here, cells, state_width), F32),
        vmem((groups, n, mixed, state_width), BF16),
        vmem((groups, n, mixed, state_width), BF16),
        vmem((groups, n, mixed, state_width), BF16),
        vmem((groups, n * mixed, channels), BF16),
        vmem((n * mixed, state_width), F32),
        vmem((groups, n, mixed, state_width), BF16),
        vmem((groups, n, mixed, state_width), BF16),
        vmem((frames_here, rows, width, state_width), BF16),
        vmem((2, chips, nz, block_a, half), BF16),
        vmem((2, nz, chips, block_b, half), BF16),
        vmem((chips, nz, block_a, half), BF16),
        vmem((nz, chips, block_b, half), BF16),
        vmem((chips - 1, nz, block_a, half), BF16),
        vmem((nz - 1, chips, block_b, half), BF16),
        vmem((chips - 1, nz, block_a, half), BF16),
        vmem((nz - 1, chips, block_b, half), BF16),
        vmem((nz, block_a, half), F32),
        vmem((chips, block_b, half), F32),
        vmem((nz, block_a, half), BF16),
        vmem((chips, block_b, half), BF16),
        vmem((nz - 1, block_a, half), BF16),
        vmem((chips - 1, block_b, half), BF16),
        vmem((n, block_a + block_b, half), BF16),
        vmem((frames_here, cells, channels), BF16),
    ]
    counts = ((2,), (n - 1,), (groups, n - 1), (groups, n - 1), (groups, n - 1), (2,))
    counts += ((chips,), (nz,), (chips - 1,), (nz - 1,), (nz - 1,), (chips - 1,))
    for count in counts + ((chips - 1,), (chips,)):
        scratch += [dma(count), dma(count)]
    spread, gathered = pl.pallas_call(
        functools.partial(fused, (n, nz, slots_a, slots_b, groups)),
        out_shape=(
            jax.ShapeDtypeStruct((frames_here, cells, channels), BF16),
            jax.ShapeDtypeStruct((n, block_a + block_b, half), BF16),
        ),
        in_specs=[hbm] * 7,
        out_specs=(hbm, hbm),
        scratch_shapes=scratch,
        compiler_params=pltpu.CompilerParams(
            collective_id=0, has_side_effects=True, vmem_limit_bytes=60 * 1024 * 1024
        ),
        cost_estimate=pl.CostEstimate(
            flops=2 * every * channels * state_width * 30,
            bytes_accessed=6 * 1024 * 1024,
            transcendentals=every * channels,
        ),
        name="conv_s5_backward",
    )(
        frames_in,
        cotangent.reshape(frames_here, cells, channels),
        kernel.reshape(9 * channels, state_width),
        readout,
        feedthrough.reshape(1, channels),
        decay_rate,
        start_state.reshape(cells, state_width),
    )
    in_a, in_b = places(slots_a)
    spread, kernel_part, readout_part = pl.pallas_call(
        functools.partial(finish, (chips, slots_a, block_a, block_b, in_a, in_b, scaling)),
        out_shape=(
            jax.ShapeDtypeStruct((frames_here, cells, channels), BF16),
            jax.ShapeDtypeStruct((9, rows_here, state_width), F32),
            jax.ShapeDtypeStruct((rows_here, state_width), F32),
        ),
        in_specs=[any_space] * 2,
        out_specs=(any_space,) * 3,
        scratch_shapes=[
            vmem((n, block_a + block_b, half), BF16),
            vmem((9, rows_here, state_width), F32),
            vmem((rows_here, state_width), F32),
            dma((4,)),
        ],
        compiler_params=pltpu.CompilerParams(vmem_limit_bytes=60 * 1024 * 1024),
        name="write_outputs",
    )(spread, gathered)
    return (spread.reshape(frames_in.shape), kernel_part, readout_part.T)


def solution(mesh):
    placed = (
        P("tm", "row", None, None),
        P("tm", "row", None, None),
        P(),
        P(),
        P(),
        P("tm", None),
        P("row", None, None),
    )
    return jax.shard_map(
        functools.partial(local, mesh.shape["tm"], mesh.shape["row"]),
        mesh=mesh,
        in_specs=placed,
        out_specs=(P("tm", "row", None, None), P(None, "row", None), P(None, "row")),
        check_vma=False,
    )
```

```python
import functools
import math

import jax
import jax.numpy as jnp
from jax import lax
from jax.experimental import pallas as pl
from jax.experimental.pallas import tpu as pltpu
from jax.sharding import PartitionSpec as P

SQRT_TWO_PI = 0.7978845608
CUBIC = 0.044715
F32 = jnp.float32
BF16 = jnp.bfloat16
MESH = pl.DeviceIdType.MESH


def gelu_slope(mixture):
    square = mixture * mixture
    tangent = jnp.tanh(SQRT_TWO_PI * (mixture + CUBIC * square * mixture))
    return 0.5 * (1.0 + tangent) + 0.5 * mixture * (1.0 - tangent * tangent) * SQRT_TWO_PI * (
        1.0 + 3.0 * CUBIC * square
    )


def place(taps, frame, padded_row, cells, rows, width):
    channels = cells.shape[1]
    wide = cells.astype(F32)
    column = lax.broadcasted_iota(jnp.int32, wide.shape, 0)
    before = jnp.where(column == 0, 0.0, pltpu.roll(wide, 1, 0)).astype(BF16)
    after = jnp.where(column == width - 1, 0.0, pltpu.roll(wide, width - 1, 0)).astype(BF16)
    for j, shifted in enumerate((before, cells, after)):
        for i in range(3):
            h = padded_row - i
            if 0 <= h < rows:
                k = 3 * i + j
                taps[
                    pl.ds((frame * rows + h) * width, width), pl.ds(k * channels, channels)
                ] = shifted


def pieces(start, size, block):
    done = 0
    while done < size:
        at = start + done
        length = min(size - done, block - at % block)
        yield at // block, at % block, done, length
        done += length


def places(slots_a):
    taps_a = min(slots_a, 9)
    in_a = {k: i for i, k in enumerate(range(9 - taps_a, 9))}
    in_b = {k: i for i, k in enumerate([9] + list(range(9 - taps_a)))}
    return in_a, in_b


def fused(
    dims,
    frames_hbm, cotangent_hbm, kernel_hbm, readout_hbm, feedthrough_hbm, decay_hbm, start_hbm,
    grad_frames, final,
    frames, cotangent, kernel, readout, feedthrough, decay, start_state, load_sems,
    taps, taps_t, drive_taps,
    halo, drive_halo, own_decay, all_decay,
    cot_send, cot_recv, driven, drv_send, drv_recv,
    states_bf, slopes, pulled, gd_send, gd_recv, drive,
    grads_a, grads_b, pair_a, pair_b, send1_a, send1_b, recv1_a, recv1_b, total_a, total_b,
    send2_a, send2_b, recv2_a, recv2_b,
    halo_ss, halo_rs, dec_ss, dec_rs, cot_ss, cot_rs, drv_ss, drv_rs, gd_ss, gd_rs,
    dhalo_ss, dhalo_rs, paira_ss, paira_rs, pairb_ss, pairb_rs, one_a_ss, one_a_rs,
    one_b_ss, one_b_rs, two_a_ss, two_a_rs, two_b_ss, two_b_rs, fin_ss, fin_rs, sib_ss, sib_rs,
):
    n, nz, slots_a, slots_b, groups = dims
    loads = [
        pltpu.make_async_copy(src, dst, load_sems.at[i])
        for i, (src, dst) in enumerate(
            (
                (decay_hbm, decay), (frames_hbm, frames), (cotangent_hbm, cotangent),
                (kernel_hbm, kernel), (start_hbm, start_state), (readout_hbm, readout),
                (feedthrough_hbm, feedthrough),
            )
        )
    ]
    for load in loads:
        load.start()
    frames_here, rows, width, channels = frames.shape
    state_width = kernel.shape[1]
    band_cells = rows * width
    share = band_cells // n
    chips = n // 2
    part_cells = share // groups
    half = state_width // 2
    me = lax.axis_index("tm")
    band = lax.axis_index("row")
    core = lax.rem(me, 2)
    chip = lax.div(me, 2)

    def remote(src, dst, send_sem, recv_sem, where):
        return pltpu.make_async_remote_copy(
            src_ref=src, dst_ref=dst, send_sem=send_sem, recv_sem=recv_sem,
            device_id=where, device_id_type=MESH,
        )

    barrier = pltpu.get_barrier_semaphore()
    for d in range(1, n):
        pl.semaphore_signal(
            barrier, inc=1, device_id={"tm": lax.rem(me + d, n)}, device_id_type=MESH
        )
    for d in range(1, nz):
        pl.semaphore_signal(
            barrier, inc=1, device_id={"row": lax.rem(band + d, nz)}, device_id_type=MESH
        )

    own_decay[...] = jnp.zeros_like(own_decay)
    loads[0].wait()
    own_decay[0:frames_here, :] = decay[...]
    all_decay[me] = own_decay[...]
    pl.semaphore_wait(barrier, (n - 1) + (nz - 1))

    def edge_copies(src, dst, ss, rs):
        up = remote(src.at[:, 0], dst.at[1], ss.at[0], rs.at[1], {"row": band - 1})
        down = remote(src.at[:, rows - 1], dst.at[0], ss.at[1], rs.at[0], {"row": band + 1})
        return up, down

    def edge_start(src, dst, ss, rs):
        up, down = edge_copies(src, dst, ss, rs)

        @pl.when(band > 0)
        def _():
            up.start()

        @pl.when(band < nz - 1)
        def _():
            down.start()

        @pl.when(band == 0)
        def _():
            dst[0] = jnp.zeros(dst.shape[1:], BF16)

        @pl.when(band == nz - 1)
        def _():
            dst[1] = jnp.zeros(dst.shape[1:], BF16)

    def edge_wait(src, dst, ss, rs, arrived):
        up, down = edge_copies(src, dst, ss, rs)

        @pl.when(band > 0)
        def _():
            if arrived:
                down.wait_recv()
            else:
                up.wait_send()

        @pl.when(band < nz - 1)
        def _():
            if arrived:
                up.wait_recv()
            else:
                down.wait_send()

    edge_start(frames_hbm, halo, halo_ss, halo_rs)
    loads[1].wait()
    loads[2].wait()
    def over_tm(src_of, dst, ss, rs):
        copies = []
        for d in range(1, n):
            to = lax.rem(me + d, n)
            copies.append(
                remote(src_of(to), dst.at[me], ss.at[d - 1], rs.at[d - 1], {"tm": to})
            )
        return copies

    def cells_of(s, g):
        begin = s * share + g * part_cells
        return slice(begin, begin + part_cells)

    for g in range(groups):
        for s in range(n):
            cot_send[g, s] = jnp.concatenate(
                [cotangent[f, cells_of(s, g), :] for f in range(frames_here)], axis=0
            )
        cot_recv[g, me] = cot_send[g, me]

    dec_copies = over_tm(lambda to: own_decay, all_decay, dec_ss, dec_rs)
    for copy in dec_copies:
        copy.start()
    cot_copies = []
    for g in range(groups):
        cot_copies.append(
            over_tm(
                lambda to, g=g: cot_send.at[g, to], cot_recv.at[g], cot_ss.at[g], cot_rs.at[g]
            )
        )
        for copy in cot_copies[g]:
            copy.start()

    for f in range(frames_here):
        for r in range(rows):
            place(taps, f, r + 1, frames[f, r], rows, width)
    edge_wait(frames_hbm, halo, halo_ss, halo_rs, True)
    for f in range(frames_here):
        place(taps, f, 0, halo[0, f], rows, width)
        place(taps, f, rows + 1, halo[1, f], rows, width)
    loads[3].wait()
    driven[...] = jnp.dot(taps[...], kernel[...], preferred_element_type=F32).reshape(driven.shape)
    drv_copies = []
    for g in range(groups):
        for s in range(n):
            drv_send[g, s] = jnp.concatenate(
                [driven[f, cells_of(s, g), :] for f in range(frames_here)], axis=0
            ).astype(BF16)
        drv_copies.append(
            over_tm(
                lambda to, g=g: drv_send.at[g, to], drv_recv.at[g], drv_ss.at[g], drv_rs.at[g]
            )
        )
        for copy in drv_copies[g]:
            copy.start()
        drv_recv[g, me] = drv_send[g, me]

    for k in range(9):
        taps_t[pl.ds(k * channels, channels), :] = taps[:, pl.ds(k * channels, channels)].T

    for load in loads[4:7]:
        load.wait()

    for copy in dec_copies:
        copy.wait_recv()
    flat = n * frames_here * part_cells
    gd_copies = []
    for g in range(groups):
        for copy in drv_copies[g]:
            copy.wait_recv()
        begin = pl.multiple_of(me * share + g * part_cells, part_cells)
        state = start_state[pl.ds(begin, part_cells), :]
        for s in range(n):
            arrived = drv_recv[g, s].astype(F32)
            kept = []
            for f in range(frames_here):
                rate = all_decay[s, f : f + 1, :]
                gain = jnp.sqrt(1.0 - rate * rate)
                state = rate * state + gain * arrived[f * part_cells : (f + 1) * part_cells]
                kept.append(state)
            states_bf[g, s] = jnp.concatenate(kept, axis=0).astype(BF16)
        for copy in cot_copies[g]:
            copy.wait_recv()
        mixture = jnp.dot(
            states_bf[g].reshape(flat, state_width), readout[...], preferred_element_type=F32
        )
        slopes[g] = (
            cot_recv[g].reshape(flat, channels).astype(F32) * gelu_slope(mixture)
        ).astype(BF16)
        pulled[...] = lax.dot_general(
            slopes[g], readout[...], (((1,), (1,)), ((), ())), preferred_element_type=F32
        )
        adjoint = jnp.zeros((part_cells, state_width), F32)
        rate = jnp.zeros((1, state_width), F32)
        for s in reversed(range(n)):
            kept = []
            for f in reversed(range(frames_here)):
                at = (s * frames_here + f) * part_cells
                adjoint = pulled[at : at + part_cells, :] + rate * adjoint
                rate = all_decay[s, f : f + 1, :]
                kept.append(jnp.sqrt(1.0 - rate * rate) * adjoint)
            gd_send[g, s] = jnp.concatenate(kept[::-1], axis=0).astype(BF16)
        gd_copies.append(
            over_tm(lambda to, g=g: gd_send.at[g, to], gd_recv.at[g], gd_ss.at[g], gd_rs.at[g])
        )
        for copy in gd_copies[g]:
            copy.start()
        gd_recv[g, me] = gd_send[g, me]

    rows_here = channels // nz
    block_a = slots_a * rows_here // chips
    block_b = slots_b * rows_here // chips
    in_a, in_b = places(slots_a)

    def keep(k, product):
        rounded = product.astype(BF16)
        part, slot, block = (
            (grads_a, in_a[k], block_a) if k in in_a else (grads_b, in_b[k], block_b)
        )
        for z in range(nz):
            for j, offset, at, length in pieces(slot * rows_here, rows_here, block):
                begin = z * rows_here + at
                place_at = (j, z) if k in in_a else (z, j)
                for h in range(2):
                    part[(h, *place_at, pl.ds(offset, length), slice(None))] = rounded[
                        begin : begin + length, h * half : (h + 1) * half
                    ]

    keep(
        9,
        lax.dot_general(
            slopes[...].reshape(groups * flat, channels),
            states_bf[...].reshape(groups * flat, state_width),
            (((0,), (0,)), ((), ())), preferred_element_type=F32
        ),
    )
    for part, slots, used, block in (
        (grads_a, slots_a, len(in_a), block_a),
        (grads_b, slots_b, len(in_b), block_b),
    ):
        if used < slots:
            for j, offset, _, length in pieces(
                used * rows_here, (slots - used) * rows_here, block
            ):
                for h in range(2):
                    for z in range(nz):
                        place_at = (j, z) if part is grads_a else (z, j)
                        part[(h, *place_at, pl.ds(offset, length), slice(None))] = jnp.zeros(
                            (length, half), BF16
                        )
    for copies in gd_copies:
        for copy in copies:
            copy.wait_recv()
    for f in range(frames_here):
        drive[f] = (
            jnp.concatenate(
                [
                    gd_recv[g, s, f * part_cells : (f + 1) * part_cells, :].astype(F32)
                    for s in range(n)
                    for g in range(groups)
                ],
                axis=0,
            )
            .astype(BF16)
            .reshape(rows, width, state_width)
        )
    edge_start(drive, drive_halo, dhalo_ss, dhalo_rs)
    flat_drive = drive[...].reshape(frames_here * band_cells, state_width)
    def tap_gradient(k):
        keep(
            k,
            jnp.dot(
                taps_t[pl.ds(k * channels, channels), :], flat_drive, preferred_element_type=F32
            ),
        )

    def over_pair(grads, pair, own, count, ss, rs):
        copies = []
        for d in list(range(1, count)) + [0]:
            at = lax.rem(own + d, count)
            copies.append(
                remote(
                    grads.at[1 - core, at], pair.at[at], ss.at[d], rs.at[d],
                    {"tm": me + 1 - 2 * core},
                )
            )
            copies[-1].start()
        return copies

    for k in range(9):
        if k in in_b:
            tap_gradient(k)
    pair_b_copies = over_pair(grads_b, pair_b, band, nz, pairb_ss, pairb_rs)
    for k in range(9):
        if k in in_a:
            tap_gradient(k)
    pair_a_copies = over_pair(grads_a, pair_a, chip, chips, paira_ss, paira_rs)

    def first_sum(pair_copies, grads, pair, own, count, send, recv, ss, rs, where, total):
        copies = []
        for d in range(1, count):
            at = lax.rem(own + d, count)
            pair_copies[d - 1].wait_recv()
            send[d - 1] = (grads[core, at].astype(F32) + pair[at].astype(F32)).astype(BF16)
            copies.append(
                remote(send.at[d - 1], recv.at[d - 1], ss.at[d - 1], rs.at[d - 1], where(at))
            )
            copies[-1].start()
        pair_copies[-1].wait_recv()
        total[...] = grads[core, own].astype(F32) + pair[own].astype(F32)
        return copies

    def to_chip(j):
        return {"tm": 2 * j + core}

    def to_band(z):
        return {"row": z}

    one_b = first_sum(
        pair_b_copies, grads_b, pair_b, band, nz, send1_b, recv1_b, one_b_ss, one_b_rs,
        to_band, total_b,
    )
    one_a = first_sum(
        pair_a_copies, grads_a, pair_a, chip, chips, send1_a, recv1_a, one_a_ss, one_a_rs,
        to_chip, total_a,
    )

    for f in range(frames_here):
        for r in range(rows):
            place(drive_taps, f, r + 1, drive[f, r], rows, width)
    edge_wait(drive, drive_halo, dhalo_ss, dhalo_rs, True)
    for f in range(frames_here):
        place(drive_taps, f, 0, drive_halo[0, f], rows, width)
        place(drive_taps, f, rows + 1, drive_halo[1, f], rows, width)
    for f in range(frames_here):
        spread = feedthrough[...] * cotangent[f].astype(F32)
        for k in range(9):
            spread = spread + lax.dot_general(
                drive_taps[
                    pl.ds(f * band_cells, band_cells), pl.ds(k * state_width, state_width)
                ],
                kernel[pl.ds((8 - k) * channels, channels), :],
                (((1,), (1,)), ((), ())),
                preferred_element_type=F32,
            )
        grad_frames[f] = spread.astype(BF16)

    def second_sum(one, recv1, total, own, count, send, recv, ss, rs, where):
        summed = total[...]
        for i, copy in enumerate(one):
            copy.wait_recv()
            summed = summed + recv1[i].astype(F32)
        total[...] = summed
        send[...] = summed.astype(BF16)
        copies = []
        for d in range(1, count):
            at = lax.rem(own + d, count)
            copies.append(
                remote(send.at[at], recv.at[d - 1], ss.at[d - 1], rs.at[d - 1], where(at))
            )
            copies[-1].start()
        return copies

    two_b = second_sum(
        one_b, recv1_b, total_b, chip, chips, send2_b, recv2_b, two_b_ss, two_b_rs, to_chip
    )
    two_a = second_sum(
        one_a, recv1_a, total_a, band, nz, send2_a, recv2_a, two_a_ss, two_a_rs, to_band
    )
    for two, recv2, total, own, begin, block in (
        (two_b, recv2_b, total_b, chip, block_a, block_b),
        (two_a, recv2_a, total_a, band, 0, block_a),
    ):
        mine = total[own]
        for i, copy in enumerate(two):
            copy.wait_recv()
            mine = mine + recv2[i].astype(F32)
        final[me, pl.ds(begin, block), :] = mine.astype(BF16)

    sibling = {"tm": me + 1 - 2 * core}
    fin_copies = []
    for d in range(1, chips):
        j = lax.rem(chip + d, chips)
        fin_copies.append(
            remote(final.at[me], final.at[me], fin_ss.at[d - 1], fin_rs.at[d - 1], to_chip(j))
        )
    sib_copies = []
    for d in range(chips):
        at = 2 * lax.rem(chip - d + chips, chips) + core
        sib_copies.append(
            remote(final.at[at], final.at[at], sib_ss.at[d], sib_rs.at[d], sibling)
        )
    for copy in fin_copies:
        copy.start()
    sib_copies[0].start()
    flat_copies = dec_copies
    for copies in cot_copies + drv_copies + gd_copies:
        flat_copies = flat_copies + copies
    for copies in (pair_a_copies, pair_b_copies, one_a, one_b, two_a, two_b):
        flat_copies = flat_copies + copies
    for copy in flat_copies:
        copy.wait_send()
    edge_wait(frames_hbm, halo, halo_ss, halo_rs, False)
    edge_wait(drive, drive_halo, dhalo_ss, dhalo_rs, False)
    for d in range(1, chips):
        fin_copies[d - 1].wait_recv()
        sib_copies[d].start()
    for copy in sib_copies:
        copy.wait_recv()
    for copy in fin_copies + sib_copies:
        copy.wait_send()


def finish(
    dims,
    spread, final, grad_frames, grad_kernel, grad_readout,
    scaled, scaled_readout, sems,
):
    chips, slots_a, block_a, block_b, in_a, in_b, scaling = dims
    rows_here, state_width = scaled_readout.shape
    half = state_width // 2
    through = pltpu.make_async_copy(spread, grad_frames, sems.at[0])
    through.start()
    for k in range(10):
        slot, block, begin = (in_a[k], block_a, 0) if k in in_a else (in_b[k], block_b, block_a)
        for j, offset, at, length in pieces(slot * rows_here, rows_here, block):
            for h in range(2):
                value = final[2 * j + h, pl.ds(begin + offset, length), :].astype(F32) * scaling
                lanes = pl.ds(h * half, half)
                if k < 9:
                    scaled[k, pl.ds(at, length), lanes] = value
                else:
                    scaled_readout[pl.ds(at, length), lanes] = value
    stores = [
        pltpu.make_async_copy(scaled, grad_kernel, sems.at[1]),
        pltpu.make_async_copy(scaled_readout, grad_readout, sems.at[2]),
    ]
    for store in stores:
        store.start()
    for copy in stores + [through]:
        copy.wait()


def local(n, nz, frames_in, cotangent, kernel, readout, feedthrough, decay_rate, start_state):
    frames_here, rows, width, channels = frames_in.shape
    state_width = kernel.shape[2]
    cells = rows * width
    share = cells // n
    chips = n // 2
    rows_here = channels // nz
    half = state_width // 2
    step = 16 * chips // math.gcd(rows_here, 16 * chips)
    slots_a = -(-7 // step) * step
    slots_b = -(-max(10 - slots_a, 1) // step) * step
    block_a = slots_a * rows_here // chips
    block_b = slots_b * rows_here // chips
    groups = 2 if frames_here * share // 2 % 16 == 0 and share % 16 == 0 else 1
    mixed = frames_here * share // groups
    scaling = 1.0 / math.sqrt(frames_here * cells * n * nz)
    vmem = pltpu.VMEM
    dma = pltpu.SemaphoreType.DMA
    any_space = pl.BlockSpec(memory_space=pl.ANY)
    whole = pl.BlockSpec(memory_space=pltpu.VMEM)
    hbm = pl.BlockSpec(memory_space=pltpu.HBM)
    every = frames_here * cells
    scratch = [
        vmem(frames_in.shape, BF16),
        vmem((frames_here, cells, channels), BF16),
        vmem((9 * channels, state_width), BF16),
        vmem(readout.shape, BF16),
        vmem((1, channels), F32),
        vmem(decay_rate.shape, F32),
        vmem((cells, state_width), F32),
        dma((7,)),
        vmem((every, 9 * channels), BF16),
        vmem((9 * channels, every), BF16),
                vmem((every, 9 * state_width), BF16),
        vmem((2, frames_here, width, channels), BF16),
        vmem((2, frames_here, width, state_width), BF16),
        vmem((8, state_width), F32),
        vmem((n, 8, state_width), F32),
        vmem((groups, n, mixed, channels), BF16),
        vmem((groups, n, mixed, channels), BF16),
        vmem((frames_here, cells, state_width), F32),
        vmem((groups, n, mixed, state_width), BF16),
        vmem((groups, n, mixed, state_width), BF16),
        vmem((groups, n, mixed, state_width), BF16),
        vmem((groups, n * mixed, channels), BF16),
        vmem((n * mixed, state_width), F32),
        vmem((groups, n, mixed, state_width), BF16),
        vmem((groups, n, mixed, state_width), BF16),
        vmem((frames_here, rows, width, state_width), BF16),
        vmem((2, chips, nz, block_a, half), BF16),
        vmem((2, nz, chips, block_b, half), BF16),
        vmem((chips, nz, block_a, half), BF16),
        vmem((nz, chips, block_b, half), BF16),
        vmem((chips - 1, nz, block_a, half), BF16),
        vmem((nz - 1, chips, block_b, half), BF16),
        vmem((chips - 1, nz, block_a, half), BF16),
        vmem((nz - 1, chips, block_b, half), BF16),
        vmem((nz, block_a, half), F32),
        vmem((chips, block_b, half), F32),
        vmem((nz, block_a, half), BF16),
        vmem((chips, block_b, half), BF16),
        vmem((nz - 1, block_a, half), BF16),
        vmem((chips - 1, block_b, half), BF16),
    ]
    counts = ((2,), (n - 1,), (groups, n - 1), (groups, n - 1), (groups, n - 1), (2,))
    counts += ((chips,), (nz,), (chips - 1,), (nz - 1,), (nz - 1,), (chips - 1,))
    for count in counts + ((chips - 1,), (chips,)):
        scratch += [dma(count), dma(count)]
    spread, gathered = pl.pallas_call(
        functools.partial(fused, (n, nz, slots_a, slots_b, groups)),
        out_shape=(
            vmem((frames_here, cells, channels), BF16),
            vmem((n, block_a + block_b, half), BF16),
        ),
        in_specs=[hbm] * 7,
        out_specs=(whole, whole),
        scratch_shapes=scratch,
        compiler_params=pltpu.CompilerParams(
            collective_id=0, has_side_effects=True, vmem_limit_bytes=48 * 1024 * 1024
        ),
        cost_estimate=pl.CostEstimate(
            flops=2 * every * channels * state_width * 30,
            bytes_accessed=6 * 1024 * 1024,
            transcendentals=every * channels,
        ),
        name="conv_s5_backward",
    )(
        *(
            pltpu.with_memory_space_constraint(argument, pltpu.HBM)
            for argument in (
                frames_in,
                cotangent.reshape(frames_here, cells, channels),
                kernel.reshape(9 * channels, state_width),
                readout,
                feedthrough.reshape(1, channels),
                decay_rate,
                start_state.reshape(cells, state_width),
            )
        )
    )
    in_a, in_b = places(slots_a)
    spread, kernel_part, readout_part = pl.pallas_call(
        functools.partial(finish, (chips, slots_a, block_a, block_b, in_a, in_b, scaling)),
        out_shape=(
            jax.ShapeDtypeStruct((frames_here, cells, channels), BF16),
            jax.ShapeDtypeStruct((9, rows_here, state_width), F32),
            jax.ShapeDtypeStruct((rows_here, state_width), F32),
        ),
        in_specs=[whole] * 2,
        out_specs=(any_space,) * 3,
        scratch_shapes=[
            vmem((9, rows_here, state_width), F32),
            vmem((rows_here, state_width), F32),
            dma((3,)),
        ],
        compiler_params=pltpu.CompilerParams(vmem_limit_bytes=48 * 1024 * 1024),
        name="write_outputs",
    )(spread, gathered)
    return (spread.reshape(frames_in.shape), kernel_part, readout_part.T)


def solution(mesh):
    placed = (
        P("tm", "row", None, None),
        P("tm", "row", None, None),
        P(),
        P(),
        P(),
        P("tm", None),
        P("row", None, None),
    )
    return jax.shard_map(
        functools.partial(local, mesh.shape["tm"], mesh.shape["row"]),
        mesh=mesh,
        in_specs=placed,
        out_specs=(P("tm", "row", None, None), P(None, "row", None), P(None, "row")),
        check_vma=False,
    )
```

```python
import functools
import math

import jax
import jax.numpy as jnp
from jax import lax
from jax.experimental import pallas as pl
from jax.experimental.pallas import tpu as pltpu
from jax.sharding import PartitionSpec as P

SQRT_TWO_PI = 0.7978845608
CUBIC = 0.044715
F32 = jnp.float32
BF16 = jnp.bfloat16
MESH = pl.DeviceIdType.MESH


def gelu_slope(mixture):
    square = mixture * mixture
    tangent = jnp.tanh(SQRT_TWO_PI * (mixture + CUBIC * square * mixture))
    return 0.5 * (1.0 + tangent) + 0.5 * mixture * (1.0 - tangent * tangent) * SQRT_TWO_PI * (
        1.0 + 3.0 * CUBIC * square
    )


def place(taps, row_at, frame, padded_row, cells, rows, width):
    channels = cells.shape[1]
    wide = cells.astype(F32)
    column = lax.broadcasted_iota(jnp.int32, wide.shape, 0)
    before = jnp.where(column == 0, 0.0, pltpu.roll(wide, 1, 0)).astype(BF16)
    after = jnp.where(column == width - 1, 0.0, pltpu.roll(wide, width - 1, 0)).astype(BF16)
    for j, shifted in enumerate((before, cells, after)):
        for i in range(3):
            h = padded_row - i
            if 0 <= h < rows:
                k = 3 * i + j
                taps[
                    pl.ds(row_at(frame, h), width), pl.ds(k * channels, channels)
                ] = shifted


def pieces(start, size, block):
    done = 0
    while done < size:
        at = start + done
        length = min(size - done, block - at % block)
        yield at // block, at % block, done, length
        done += length


def places(slots_a):
    taps_a = min(slots_a, 9)
    in_a = {k: i for i, k in enumerate(range(9 - taps_a, 9))}
    in_b = {k: i for i, k in enumerate([9] + list(range(9 - taps_a)))}
    return in_a, in_b


def fused(
    dims,
    frames_hbm, cotangent_hbm, kernel_hbm, readout_hbm, feedthrough_hbm, decay_hbm, start_hbm,
    grad_frames, final,
    frames, cotangent, kernel, readout, feedthrough, decay, start_state, load_sems,
    taps, taps_t, drive_taps,
    halo, drive_halo, own_decay, all_decay,
    cot_send, cot_recv, driven, drv_send, drv_recv,
    states_bf, slopes, pulled, gd_send, gd_recv, drive, drive_flat,
    grads_a, grads_b, pair_a, pair_b, send1_a, send1_b, recv1_a, recv1_b, total_a, total_b,
    send2_a, send2_b, recv2_a, recv2_b,
    halo_ss, halo_rs, dec_ss, dec_rs, cot_ss, cot_rs, drv_ss, drv_rs, gd_ss, gd_rs,
    dhalo_ss, dhalo_rs, paira_ss, paira_rs, pairb_ss, pairb_rs, one_a_ss, one_a_rs,
    one_b_ss, one_b_rs, two_a_ss, two_a_rs, two_b_ss, two_b_rs, fin_ss, fin_rs, sib_ss, sib_rs,
):
    n, nz, slots_a, slots_b, groups = dims
    loads = [
        pltpu.make_async_copy(src, dst, load_sems.at[i])
        for i, (src, dst) in enumerate(
            (
                (decay_hbm, decay), (frames_hbm, frames), (cotangent_hbm, cotangent),
                (kernel_hbm, kernel), (start_hbm, start_state), (readout_hbm, readout),
                (feedthrough_hbm, feedthrough),
            )
        )
    ]
    for load in loads:
        load.start()
    frames_here, rows, width, channels = frames.shape
    state_width = kernel.shape[1]
    band_cells = rows * width
    share = band_cells // n
    chips = n // 2
    part_cells = share // groups
    half = state_width // 2
    me = lax.axis_index("tm")
    band = lax.axis_index("row")
    core = lax.rem(me, 2)
    chip = lax.div(me, 2)

    def remote(src, dst, send_sem, recv_sem, where):
        return pltpu.make_async_remote_copy(
            src_ref=src, dst_ref=dst, send_sem=send_sem, recv_sem=recv_sem,
            device_id=where, device_id_type=MESH,
        )

    barrier = pltpu.get_barrier_semaphore()
    for d in range(1, n):
        pl.semaphore_signal(
            barrier, inc=1, device_id={"tm": lax.rem(me + d, n)}, device_id_type=MESH
        )
    for d in range(1, nz):
        pl.semaphore_signal(
            barrier, inc=1, device_id={"row": lax.rem(band + d, nz)}, device_id_type=MESH
        )

    own_decay[...] = jnp.zeros_like(own_decay)
    loads[0].wait()
    own_decay[0:frames_here, :] = decay[...]
    all_decay[me] = own_decay[...]
    pl.semaphore_wait(barrier, (n - 1) + (nz - 1))

    def edge_copies(src, dst, ss, rs):
        up = remote(src.at[:, 0], dst.at[1], ss.at[0], rs.at[1], {"row": band - 1})
        down = remote(src.at[:, rows - 1], dst.at[0], ss.at[1], rs.at[0], {"row": band + 1})
        return up, down

    def edge_start(src, dst, ss, rs):
        up, down = edge_copies(src, dst, ss, rs)

        @pl.when(band > 0)
        def _():
            up.start()

        @pl.when(band < nz - 1)
        def _():
            down.start()

        @pl.when(band == 0)
        def _():
            dst[0] = jnp.zeros(dst.shape[1:], BF16)

        @pl.when(band == nz - 1)
        def _():
            dst[1] = jnp.zeros(dst.shape[1:], BF16)

    def edge_wait(src, dst, ss, rs, arrived):
        up, down = edge_copies(src, dst, ss, rs)

        @pl.when(band > 0)
        def _():
            if arrived:
                down.wait_recv()
            else:
                up.wait_send()

        @pl.when(band < nz - 1)
        def _():
            if arrived:
                up.wait_recv()
            else:
                down.wait_send()

    edge_start(frames_hbm, halo, halo_ss, halo_rs)
    loads[1].wait()
    def over_tm(src_of, dst, ss, rs):
        copies = []
        for d in range(1, n):
            to = lax.rem(me + d, n)
            copies.append(
                remote(src_of(to), dst.at[me], ss.at[d - 1], rs.at[d - 1], {"tm": to})
            )
        return copies

    group_cells = band_cells // groups
    group_rows = rows // groups

    def cells_of(s, g):
        begin = g * group_cells + s * part_cells
        return slice(begin, begin + part_cells)

    def row_at(f, h):
        return ((h // group_rows * frames_here + f) * group_rows + h % group_rows) * width

    def in_group(g):
        return pl.ds(g * frames_here * group_cells, frames_here * group_cells)


    dec_copies = over_tm(lambda to: own_decay, all_decay, dec_ss, dec_rs)
    for copy in dec_copies:
        copy.start()
    for f in range(frames_here):
        for r in range(rows):
            place(taps, row_at, f, r + 1, frames[f, r], rows, width)
    loads[2].wait()
    for s in range(n):
        for g in range(groups):
            cot_send[s, g] = jnp.concatenate(
                [cotangent[f, cells_of(s, g), :] for f in range(frames_here)], axis=0
            )
    cot_copies = over_tm(lambda to: cot_send.at[to], cot_recv, cot_ss, cot_rs)
    for copy in cot_copies:
        copy.start()
    cot_recv[me] = cot_send[me]
    edge_wait(frames_hbm, halo, halo_ss, halo_rs, True)
    for f in range(frames_here):
        place(taps, row_at, f, 0, halo[0, f], rows, width)
        place(taps, row_at, f, rows + 1, halo[1, f], rows, width)
    loads[3].wait()
    drv_copies = []
    for g in range(groups):
        driven[g] = jnp.dot(
            taps[in_group(g), :], kernel[...], preferred_element_type=F32
        ).reshape(driven.shape[1:])
        for s in range(n):
            drv_send[g, s] = jnp.concatenate(
                [
                    driven[g, f, s * part_cells : (s + 1) * part_cells, :]
                    for f in range(frames_here)
                ],
                axis=0,
            ).astype(BF16)
        drv_copies.append(
            over_tm(
                lambda to, g=g: drv_send.at[g, to], drv_recv.at[g], drv_ss.at[g], drv_rs.at[g]
            )
        )
        for copy in drv_copies[g]:
            copy.start()
        drv_recv[g, me] = drv_send[g, me]

    def transpose_taps(first, last):
        for k in range(first, last):
            taps_t[pl.ds(k * channels, channels), :] = taps[:, pl.ds(k * channels, channels)].T

    transpose_taps(0, 4)
    for load in loads[4:7]:
        load.wait()

    for copy in dec_copies:
        copy.wait_recv()
    flat = n * frames_here * part_cells
    gd_copies = []
    for g in range(groups):
        for copy in drv_copies[g]:
            copy.wait_recv()
        begin = pl.multiple_of(g * group_cells + me * part_cells, part_cells)
        state = start_state[pl.ds(begin, part_cells), :]
        for s in range(n):
            arrived = drv_recv[g, s].astype(F32)
            kept = []
            for f in range(frames_here):
                rate = all_decay[s, f : f + 1, :]
                gain = jnp.sqrt(1.0 - rate * rate)
                state = rate * state + gain * arrived[f * part_cells : (f + 1) * part_cells]
                kept.append(state)
            states_bf[g, s] = jnp.concatenate(kept, axis=0).astype(BF16)
        if g == 0:
            for copy in cot_copies:
                copy.wait_recv()
        mixture = jnp.dot(
            states_bf[g].reshape(flat, state_width), readout[...], preferred_element_type=F32
        )
        slopes[g] = (
            cot_recv[:, g].reshape(flat, channels).astype(F32) * gelu_slope(mixture)
        ).astype(BF16)
        pulled[...] = lax.dot_general(
            slopes[g], readout[...], (((1,), (1,)), ((), ())), preferred_element_type=F32
        )
        adjoint = jnp.zeros((part_cells, state_width), F32)
        rate = jnp.zeros((1, state_width), F32)
        for s in reversed(range(n)):
            kept = []
            for f in reversed(range(frames_here)):
                at = (s * frames_here + f) * part_cells
                adjoint = pulled[at : at + part_cells, :] + rate * adjoint
                rate = all_decay[s, f : f + 1, :]
                kept.append(jnp.sqrt(1.0 - rate * rate) * adjoint)
            gd_send[g, s] = jnp.concatenate(kept[::-1], axis=0).astype(BF16)
        gd_copies.append(
            over_tm(lambda to, g=g: gd_send.at[g, to], gd_recv.at[g], gd_ss.at[g], gd_rs.at[g])
        )
        for copy in gd_copies[g]:
            copy.start()
        gd_recv[g, me] = gd_send[g, me]

    rows_here = channels // nz
    block_a = slots_a * rows_here // chips
    block_b = slots_b * rows_here // chips
    in_a, in_b = places(slots_a)

    def keep(k, product):
        rounded = product.astype(BF16)
        part, slot, block = (
            (grads_a, in_a[k], block_a) if k in in_a else (grads_b, in_b[k], block_b)
        )
        for z in range(nz):
            for j, offset, at, length in pieces(slot * rows_here, rows_here, block):
                begin = z * rows_here + at
                place_at = (j, z) if k in in_a else (z, j)
                for h in range(2):
                    part[(h, *place_at, pl.ds(offset, length), slice(None))] = rounded[
                        begin : begin + length, h * half : (h + 1) * half
                    ]

    keep(
        9,
        lax.dot_general(
            slopes[...].reshape(groups * flat, channels),
            states_bf[...].reshape(groups * flat, state_width),
            (((0,), (0,)), ((), ())), preferred_element_type=F32
        ),
    )
    for part, slots, used, block in (
        (grads_a, slots_a, len(in_a), block_a),
        (grads_b, slots_b, len(in_b), block_b),
    ):
        if used < slots:
            for j, offset, _, length in pieces(
                used * rows_here, (slots - used) * rows_here, block
            ):
                for h in range(2):
                    for z in range(nz):
                        place_at = (j, z) if part is grads_a else (z, j)
                        part[(h, *place_at, pl.ds(offset, length), slice(None))] = jnp.zeros(
                            (length, half), BF16
                        )
    transpose_taps(4, 9)
    for copies in gd_copies:
        for copy in copies:
            copy.wait_recv()
    for g in range(groups):
        for f in range(frames_here):
            back = jnp.concatenate(
                [
                    gd_recv[g, s, f * part_cells : (f + 1) * part_cells, :].astype(F32)
                    for s in range(n)
                ],
                axis=0,
            ).astype(BF16)
            drive_flat[pl.ds((g * frames_here + f) * group_cells, group_cells), :] = back
            drive[f, g * group_rows : (g + 1) * group_rows] = back.reshape(
                group_rows, width, state_width
            )
    edge_start(drive, drive_halo, dhalo_ss, dhalo_rs)
    flat_drive = drive_flat[...]

    def tap_gradient(k):
        keep(
            k,
            jnp.dot(
                taps_t[pl.ds(k * channels, channels), :], flat_drive, preferred_element_type=F32
            ),
        )

    def over_pair(grads, pair, own, count, ss, rs):
        copies = []
        for d in list(range(1, count)) + [0]:
            at = lax.rem(own + d, count)
            copies.append(
                remote(
                    grads.at[1 - core, at], pair.at[at], ss.at[d], rs.at[d],
                    {"tm": me + 1 - 2 * core},
                )
            )
            copies[-1].start()
        return copies

    for k in range(9):
        if k in in_b:
            tap_gradient(k)
    pair_b_copies = over_pair(grads_b, pair_b, band, nz, pairb_ss, pairb_rs)
    for k in range(9):
        if k in in_a:
            tap_gradient(k)
    pair_a_copies = over_pair(grads_a, pair_a, chip, chips, paira_ss, paira_rs)

    def first_sum(pair_copies, grads, pair, own, count, send, recv, ss, rs, where, total):
        copies = []
        for d in range(1, count):
            at = lax.rem(own + d, count)
            pair_copies[d - 1].wait_recv()
            send[d - 1] = (grads[core, at].astype(F32) + pair[at].astype(F32)).astype(BF16)
            copies.append(
                remote(send.at[d - 1], recv.at[d - 1], ss.at[d - 1], rs.at[d - 1], where(at))
            )
            copies[-1].start()
        pair_copies[-1].wait_recv()
        total[...] = grads[core, own].astype(F32) + pair[own].astype(F32)
        return copies

    def to_chip(j):
        return {"tm": 2 * j + core}

    def to_band(z):
        return {"row": z}

    one_b = first_sum(
        pair_b_copies, grads_b, pair_b, band, nz, send1_b, recv1_b, one_b_ss, one_b_rs,
        to_band, total_b,
    )
    one_a = first_sum(
        pair_a_copies, grads_a, pair_a, chip, chips, send1_a, recv1_a, one_a_ss, one_a_rs,
        to_chip, total_a,
    )

    for f in range(frames_here):
        for r in range(rows):
            place(drive_taps, row_at, f, r + 1, drive[f, r], rows, width)
    edge_wait(drive, drive_halo, dhalo_ss, dhalo_rs, True)
    for f in range(frames_here):
        place(drive_taps, row_at, f, 0, drive_halo[0, f], rows, width)
        place(drive_taps, row_at, f, rows + 1, drive_halo[1, f], rows, width)
    for g in range(groups):
        spread = jnp.concatenate(
            [
                feedthrough[...]
                * cotangent[f, g * group_cells : (g + 1) * group_cells, :].astype(F32)
                for f in range(frames_here)
            ],
            axis=0,
        )
        for k in range(9):
            spread = spread + lax.dot_general(
                drive_taps[in_group(g), pl.ds(k * state_width, state_width)],
                kernel[pl.ds((8 - k) * channels, channels), :],
                (((1,), (1,)), ((), ())),
                preferred_element_type=F32,
            )
        for f in range(frames_here):
            grad_frames[f, g * group_cells : (g + 1) * group_cells, :] = spread[
                f * group_cells : (f + 1) * group_cells
            ].astype(BF16)

    def second_sum(one, recv1, total, own, count, send, recv, ss, rs, where):
        summed = total[...]
        for i, copy in enumerate(one):
            copy.wait_recv()
            summed = summed + recv1[i].astype(F32)
        total[...] = summed
        send[...] = summed.astype(BF16)
        copies = []
        for d in range(1, count):
            at = lax.rem(own + d, count)
            copies.append(
                remote(send.at[at], recv.at[d - 1], ss.at[d - 1], rs.at[d - 1], where(at))
            )
            copies[-1].start()
        return copies

    two_b = second_sum(
        one_b, recv1_b, total_b, chip, chips, send2_b, recv2_b, two_b_ss, two_b_rs, to_chip
    )
    two_a = second_sum(
        one_a, recv1_a, total_a, band, nz, send2_a, recv2_a, two_a_ss, two_a_rs, to_band
    )
    for two, recv2, total, own, begin, block in (
        (two_b, recv2_b, total_b, chip, block_a, block_b),
        (two_a, recv2_a, total_a, band, 0, block_a),
    ):
        mine = total[own]
        for i, copy in enumerate(two):
            copy.wait_recv()
            mine = mine + recv2[i].astype(F32)
        final[me, pl.ds(begin, block), :] = mine.astype(BF16)

    sibling = {"tm": me + 1 - 2 * core}
    fin_copies = []
    for d in range(1, chips):
        j = lax.rem(chip + d, chips)
        fin_copies.append(
            remote(final.at[me], final.at[me], fin_ss.at[d - 1], fin_rs.at[d - 1], to_chip(j))
        )
    sib_copies = []
    for d in range(chips):
        at = 2 * lax.rem(chip - d + chips, chips) + core
        sib_copies.append(
            remote(final.at[at], final.at[at], sib_ss.at[d], sib_rs.at[d], sibling)
        )
    for copy in fin_copies:
        copy.start()
    sib_copies[0].start()
    flat_copies = dec_copies
    for copies in [cot_copies] + drv_copies + gd_copies:
        flat_copies = flat_copies + copies
    for copies in (pair_a_copies, pair_b_copies, one_a, one_b, two_a, two_b):
        flat_copies = flat_copies + copies
    for copy in flat_copies:
        copy.wait_send()
    edge_wait(frames_hbm, halo, halo_ss, halo_rs, False)
    edge_wait(drive, drive_halo, dhalo_ss, dhalo_rs, False)
    for d in range(1, chips):
        fin_copies[d - 1].wait_recv()
        sib_copies[d].start()
    for copy in sib_copies:
        copy.wait_recv()
    for copy in fin_copies + sib_copies:
        copy.wait_send()


def finish(
    dims,
    spread, final, grad_frames, grad_kernel, grad_readout,
    scaled, scaled_readout, sems,
):
    chips, slots_a, block_a, block_b, in_a, in_b, scaling = dims
    rows_here, state_width = scaled_readout.shape
    half = state_width // 2
    through = pltpu.make_async_copy(spread, grad_frames, sems.at[0])
    through.start()
    for k in range(10):
        slot, block, begin = (in_a[k], block_a, 0) if k in in_a else (in_b[k], block_b, block_a)
        for j, offset, at, length in pieces(slot * rows_here, rows_here, block):
            for h in range(2):
                value = final[2 * j + h, pl.ds(begin + offset, length), :].astype(F32) * scaling
                lanes = pl.ds(h * half, half)
                if k < 9:
                    scaled[k, pl.ds(at, length), lanes] = value
                else:
                    scaled_readout[pl.ds(at, length), lanes] = value
    stores = [
        pltpu.make_async_copy(scaled, grad_kernel, sems.at[1]),
        pltpu.make_async_copy(scaled_readout, grad_readout, sems.at[2]),
    ]
    for store in stores:
        store.start()
    for copy in stores + [through]:
        copy.wait()


def local(n, nz, frames_in, cotangent, kernel, readout, feedthrough, decay_rate, start_state):
    frames_here, rows, width, channels = frames_in.shape
    state_width = kernel.shape[2]
    cells = rows * width
    share = cells // n
    chips = n // 2
    rows_here = channels // nz
    half = state_width // 2
    step = 16 * chips // math.gcd(rows_here, 16 * chips)
    slots_a = -(-7 // step) * step
    slots_b = -(-max(10 - slots_a, 1) // step) * step
    block_a = slots_a * rows_here // chips
    block_b = slots_b * rows_here // chips
    groups = 2 if frames_here * share // 2 % 16 == 0 and share % 16 == 0 and rows % 2 == 0 else 1
    mixed = frames_here * share // groups
    scaling = 1.0 / math.sqrt(frames_here * cells * n * nz)
    vmem = pltpu.VMEM
    dma = pltpu.SemaphoreType.DMA
    any_space = pl.BlockSpec(memory_space=pl.ANY)
    whole = pl.BlockSpec(memory_space=pltpu.VMEM)
    hbm = pl.BlockSpec(memory_space=pltpu.HBM)
    every = frames_here * cells
    scratch = [
        vmem(frames_in.shape, BF16),
        vmem((frames_here, cells, channels), BF16),
        vmem((9 * channels, state_width), BF16),
        vmem(readout.shape, BF16),
        vmem((1, channels), F32),
        vmem(decay_rate.shape, F32),
        vmem((cells, state_width), F32),
        dma((7,)),
        vmem((every, 9 * channels), BF16),
        vmem((9 * channels, every), BF16),
                vmem((every, 9 * state_width), BF16),
        vmem((2, frames_here, width, channels), BF16),
        vmem((2, frames_here, width, state_width), BF16),
        vmem((8, state_width), F32),
        vmem((n, 8, state_width), F32),
        vmem((n, groups, mixed, channels), BF16),
        vmem((n, groups, mixed, channels), BF16),
        vmem((groups, frames_here, cells // groups, state_width), F32),
        vmem((groups, n, mixed, state_width), BF16),
        vmem((groups, n, mixed, state_width), BF16),
        vmem((groups, n, mixed, state_width), BF16),
        vmem((groups, n * mixed, channels), BF16),
        vmem((n * mixed, state_width), F32),
        vmem((groups, n, mixed, state_width), BF16),
        vmem((groups, n, mixed, state_width), BF16),
        vmem((frames_here, rows, width, state_width), BF16),
        vmem((every, state_width), BF16),
        vmem((2, chips, nz, block_a, half), BF16),
        vmem((2, nz, chips, block_b, half), BF16),
        vmem((chips, nz, block_a, half), BF16),
        vmem((nz, chips, block_b, half), BF16),
        vmem((chips - 1, nz, block_a, half), BF16),
        vmem((nz - 1, chips, block_b, half), BF16),
        vmem((chips - 1, nz, block_a, half), BF16),
        vmem((nz - 1, chips, block_b, half), BF16),
        vmem((nz, block_a, half), F32),
        vmem((chips, block_b, half), F32),
        vmem((nz, block_a, half), BF16),
        vmem((chips, block_b, half), BF16),
        vmem((nz - 1, block_a, half), BF16),
        vmem((chips - 1, block_b, half), BF16),
    ]
    counts = ((2,), (n - 1,), (n - 1,), (groups, n - 1), (groups, n - 1), (2,))
    counts += ((chips,), (nz,), (chips - 1,), (nz - 1,), (nz - 1,), (chips - 1,))
    for count in counts + ((chips - 1,), (chips,)):
        scratch += [dma(count), dma(count)]
    spread, gathered = pl.pallas_call(
        functools.partial(fused, (n, nz, slots_a, slots_b, groups)),
        out_shape=(
            vmem((frames_here, cells, channels), BF16),
            vmem((n, block_a + block_b, half), BF16),
        ),
        in_specs=[hbm] * 7,
        out_specs=(whole, whole),
        scratch_shapes=scratch,
        compiler_params=pltpu.CompilerParams(
            collective_id=0, has_side_effects=True, vmem_limit_bytes=48 * 1024 * 1024
        ),
        cost_estimate=pl.CostEstimate(
            flops=2 * every * channels * state_width * 30,
            bytes_accessed=6 * 1024 * 1024,
            transcendentals=every * channels,
        ),
        name="conv_s5_backward",
    )(
        *(
            pltpu.with_memory_space_constraint(argument, pltpu.HBM)
            for argument in (
                frames_in,
                cotangent.reshape(frames_here, cells, channels),
                kernel.reshape(9 * channels, state_width),
                readout,
                feedthrough.reshape(1, channels),
                decay_rate,
                start_state.reshape(cells, state_width),
            )
        )
    )
    in_a, in_b = places(slots_a)
    spread, kernel_part, readout_part = pl.pallas_call(
        functools.partial(finish, (chips, slots_a, block_a, block_b, in_a, in_b, scaling)),
        out_shape=(
            jax.ShapeDtypeStruct((frames_here, cells, channels), BF16),
            jax.ShapeDtypeStruct((9, rows_here, state_width), F32),
            jax.ShapeDtypeStruct((rows_here, state_width), F32),
        ),
        in_specs=[whole] * 2,
        out_specs=(any_space,) * 3,
        scratch_shapes=[
            vmem((9, rows_here, state_width), F32),
            vmem((rows_here, state_width), F32),
            dma((3,)),
        ],
        compiler_params=pltpu.CompilerParams(vmem_limit_bytes=48 * 1024 * 1024),
        name="write_outputs",
    )(spread, gathered)
    return (spread.reshape(frames_in.shape), kernel_part, readout_part.T)


def solution(mesh):
    placed = (
        P("tm", "row", None, None),
        P("tm", "row", None, None),
        P(),
        P(),
        P(),
        P("tm", None),
        P("row", None, None),
    )
    return jax.shard_map(
        functools.partial(local, mesh.shape["tm"], mesh.shape["row"]),
        mesh=mesh,
        in_specs=placed,
        out_specs=(P("tm", "row", None, None), P(None, "row", None), P(None, "row")),
        check_vma=False,
    )
```

```python
import functools
import math

import jax
import jax.numpy as jnp
from jax import lax
from jax.experimental import pallas as pl
from jax.experimental.pallas import tpu as pltpu
from jax.sharding import PartitionSpec as P

SQRT_TWO_PI = 0.7978845608
CUBIC = 0.044715
F32 = jnp.float32
BF16 = jnp.bfloat16
MESH = pl.DeviceIdType.MESH


def gelu_slope(mixture):
    square = mixture * mixture
    tangent = jnp.tanh(SQRT_TWO_PI * (mixture + CUBIC * square * mixture))
    return 0.5 * (1.0 + tangent) + 0.5 * mixture * (1.0 - tangent * tangent) * SQRT_TWO_PI * (
        1.0 + 3.0 * CUBIC * square
    )


def place(taps, row_at, frame, padded_row, cells, rows, width):
    channels = cells.shape[1]
    wide = cells.astype(F32)
    column = lax.broadcasted_iota(jnp.int32, wide.shape, 0)
    before = jnp.where(column == 0, 0.0, pltpu.roll(wide, 1, 0)).astype(BF16)
    after = jnp.where(column == width - 1, 0.0, pltpu.roll(wide, width - 1, 0)).astype(BF16)
    for j, shifted in enumerate((before, cells, after)):
        for i in range(3):
            h = padded_row - i
            if 0 <= h < rows:
                k = 3 * i + j
                taps[
                    pl.ds(row_at(frame, h), width), pl.ds(k * channels, channels)
                ] = shifted


def pieces(start, size, block):
    done = 0
    while done < size:
        at = start + done
        length = min(size - done, block - at % block)
        yield at // block, at % block, done, length
        done += length


def places(slots_a):
    taps_a = min(slots_a, 9)
    in_a = {k: i for i, k in enumerate(range(9 - taps_a, 9))}
    in_b = {k: i for i, k in enumerate([9] + list(range(9 - taps_a)))}
    return in_a, in_b


def fused(
    dims,
    frames_hbm, cotangent_hbm, kernel_hbm, readout_hbm, feedthrough_hbm, decay_hbm, start_hbm,
    grad_frames, final,
    frames, cotangent, kernel, readout, feedthrough, decay, start_state, load_sems,
    taps, taps_t, drive_taps,
    halo, drive_halo, own_decay, all_decay,
    cot_send, cot_recv, driven, drv_send, drv_recv,
    states_bf, slopes, pulled, gd_send, gd_recv, drive, drive_flat,
    grads_a, grads_b, pair_a, pair_b, send1_a, send1_b, recv1_a, recv1_b, total_a, total_b,
    send2_a, send2_b, recv2_a, recv2_b,
    halo_ss, halo_rs, dec_ss, dec_rs, cot_ss, cot_rs, drv_ss, drv_rs, gd_ss, gd_rs,
    dhalo_ss, dhalo_rs, paira_ss, paira_rs, pairb_ss, pairb_rs, one_a_ss, one_a_rs,
    one_b_ss, one_b_rs, two_a_ss, two_a_rs, two_b_ss, two_b_rs, fin_ss, fin_rs, sib_ss, sib_rs,
):
    n, nz, slots_a, slots_b, groups = dims
    loads = [
        pltpu.make_async_copy(src, dst, load_sems.at[i])
        for i, (src, dst) in enumerate(
            (
                (decay_hbm, decay), (frames_hbm, frames), (cotangent_hbm, cotangent),
                (kernel_hbm, kernel), (start_hbm, start_state), (readout_hbm, readout),
                (feedthrough_hbm, feedthrough),
            )
        )
    ]
    for load in loads:
        load.start()
    frames_here, rows, width, channels = frames.shape
    state_width = kernel.shape[1]
    band_cells = rows * width
    share = band_cells // n
    chips = n // 2
    part_cells = share // groups
    half = state_width // 2
    me = lax.axis_index("tm")
    band = lax.axis_index("row")
    core = lax.rem(me, 2)
    chip = lax.div(me, 2)

    def remote(src, dst, send_sem, recv_sem, where):
        return pltpu.make_async_remote_copy(
            src_ref=src, dst_ref=dst, send_sem=send_sem, recv_sem=recv_sem,
            device_id=where, device_id_type=MESH,
        )

    barrier = pltpu.get_barrier_semaphore()
    for d in range(1, n):
        pl.semaphore_signal(
            barrier, inc=1, device_id={"tm": lax.rem(me + d, n)}, device_id_type=MESH
        )
    for d in range(1, nz):
        pl.semaphore_signal(
            barrier, inc=1, device_id={"row": lax.rem(band + d, nz)}, device_id_type=MESH
        )

    own_decay[...] = jnp.zeros_like(own_decay)
    loads[0].wait()
    own_decay[0:frames_here, :] = decay[...]
    all_decay[me] = own_decay[...]
    pl.semaphore_wait(barrier, (n - 1) + (nz - 1))

    def edge_copies(src, dst, ss, rs):
        up = remote(src.at[:, 0], dst.at[1], ss.at[0], rs.at[1], {"row": band - 1})
        down = remote(src.at[:, rows - 1], dst.at[0], ss.at[1], rs.at[0], {"row": band + 1})
        return up, down

    def edge_start(src, dst, ss, rs):
        up, down = edge_copies(src, dst, ss, rs)

        @pl.when(band > 0)
        def _():
            up.start()

        @pl.when(band < nz - 1)
        def _():
            down.start()

        @pl.when(band == 0)
        def _():
            dst[0] = jnp.zeros(dst.shape[1:], BF16)

        @pl.when(band == nz - 1)
        def _():
            dst[1] = jnp.zeros(dst.shape[1:], BF16)

    def edge_wait(src, dst, ss, rs, arrived):
        up, down = edge_copies(src, dst, ss, rs)

        @pl.when(band > 0)
        def _():
            if arrived:
                down.wait_recv()
            else:
                up.wait_send()

        @pl.when(band < nz - 1)
        def _():
            if arrived:
                up.wait_recv()
            else:
                down.wait_send()

    edge_start(frames_hbm, halo, halo_ss, halo_rs)
    loads[1].wait()
    def over_tm(src_of, dst, ss, rs):
        copies = []
        for d in range(1, n):
            to = lax.rem(me + d, n)
            copies.append(
                remote(src_of(to), dst.at[me], ss.at[d - 1], rs.at[d - 1], {"tm": to})
            )
        return copies

    group_cells = band_cells // groups
    group_rows = rows // groups

    def cells_of(s, g):
        begin = g * group_cells + s * part_cells
        return slice(begin, begin + part_cells)

    def row_at(f, h):
        return ((h // group_rows * frames_here + f) * group_rows + h % group_rows) * width

    def in_group(g):
        return pl.ds(g * frames_here * group_cells, frames_here * group_cells)


    dec_copies = over_tm(lambda to: own_decay, all_decay, dec_ss, dec_rs)
    for copy in dec_copies:
        copy.start()
    for f in range(frames_here):
        for r in range(rows):
            place(taps, row_at, f, r + 1, frames[f, r], rows, width)
    loads[2].wait()
    for s in range(n):
        for g in range(groups):
            cot_send[s, g] = jnp.concatenate(
                [cotangent[f, cells_of(s, g), :] for f in range(frames_here)], axis=0
            )
    cot_copies = over_tm(lambda to: cot_send.at[to], cot_recv, cot_ss, cot_rs)
    for copy in cot_copies:
        copy.start()
    cot_recv[me] = cot_send[me]
    rim_taps = ((0, 0, pl.ds(0, 3 * channels)), (1, rows - 1, pl.ds(6 * channels, 3 * channels)))
    for _, h, columns in rim_taps:
        for f in range(frames_here):
            taps[pl.ds(row_at(f, h), width), columns] = jnp.zeros((width, 3 * channels), BF16)
    loads[3].wait()
    for g in range(groups):
        driven[g] = jnp.dot(
            taps[in_group(g), :], kernel[...], preferred_element_type=F32
        ).reshape(driven.shape[1:])
    edge_wait(frames_hbm, halo, halo_ss, halo_rs, True)
    for f in range(frames_here):
        place(taps, row_at, f, 0, halo[0, f], rows, width)
        place(taps, row_at, f, rows + 1, halo[1, f], rows, width)
    drv_copies = []
    for g in range(groups):
        for _, h, columns in rim_taps:
            if h // group_rows == g:
                rim = jnp.concatenate(
                    [taps[pl.ds(row_at(f, h), width), columns] for f in range(frames_here)], axis=0
                )
                added = jnp.dot(rim, kernel[columns, :], preferred_element_type=F32)
                at = pl.ds(h % group_rows * width, width)
                for f in range(frames_here):
                    driven[g, f, at, :] += added[f * width : (f + 1) * width]
        for s in range(n):
            drv_send[g, s] = jnp.concatenate(
                [
                    driven[g, f, s * part_cells : (s + 1) * part_cells, :]
                    for f in range(frames_here)
                ],
                axis=0,
            ).astype(BF16)
        drv_copies.append(
            over_tm(
                lambda to, g=g: drv_send.at[g, to], drv_recv.at[g], drv_ss.at[g], drv_rs.at[g]
            )
        )
        for copy in drv_copies[g]:
            copy.start()
        drv_recv[g, me] = drv_send[g, me]

    def transpose_taps(first, last):
        for k in range(first, last):
            taps_t[pl.ds(k * channels, channels), :] = taps[:, pl.ds(k * channels, channels)].T

    transpose_taps(0, 4)
    for load in loads[4:7]:
        load.wait()

    for copy in dec_copies:
        copy.wait_recv()
    flat = n * frames_here * part_cells
    gd_copies = []
    for g in range(groups):
        for copy in drv_copies[g]:
            copy.wait_recv()
        begin = pl.multiple_of(g * group_cells + me * part_cells, part_cells)
        state = start_state[pl.ds(begin, part_cells), :]
        for s in range(n):
            arrived = drv_recv[g, s].astype(F32)
            kept = []
            for f in range(frames_here):
                rate = all_decay[s, f : f + 1, :]
                gain = jnp.sqrt(1.0 - rate * rate)
                state = rate * state + gain * arrived[f * part_cells : (f + 1) * part_cells]
                kept.append(state)
            states_bf[g, s] = jnp.concatenate(kept, axis=0).astype(BF16)
        if g == 0:
            for copy in cot_copies:
                copy.wait_recv()
        mixture = jnp.dot(
            states_bf[g].reshape(flat, state_width), readout[...], preferred_element_type=F32
        )
        slopes[g] = (
            cot_recv[:, g].reshape(flat, channels).astype(F32) * gelu_slope(mixture)
        ).astype(BF16)
        pulled[...] = lax.dot_general(
            slopes[g], readout[...], (((1,), (1,)), ((), ())), preferred_element_type=F32
        )
        adjoint = jnp.zeros((part_cells, state_width), F32)
        rate = jnp.zeros((1, state_width), F32)
        for s in reversed(range(n)):
            kept = []
            for f in reversed(range(frames_here)):
                at = (s * frames_here + f) * part_cells
                adjoint = pulled[at : at + part_cells, :] + rate * adjoint
                rate = all_decay[s, f : f + 1, :]
                kept.append(jnp.sqrt(1.0 - rate * rate) * adjoint)
            gd_send[g, s] = jnp.concatenate(kept[::-1], axis=0).astype(BF16)
        gd_copies.append(
            over_tm(lambda to, g=g: gd_send.at[g, to], gd_recv.at[g], gd_ss.at[g], gd_rs.at[g])
        )
        for copy in gd_copies[g]:
            copy.start()
        gd_recv[g, me] = gd_send[g, me]

    rows_here = channels // nz
    block_a = slots_a * rows_here // chips
    block_b = slots_b * rows_here // chips
    in_a, in_b = places(slots_a)

    def keep(k, product):
        rounded = product.astype(BF16)
        part, slot, block = (
            (grads_a, in_a[k], block_a) if k in in_a else (grads_b, in_b[k], block_b)
        )
        for z in range(nz):
            for j, offset, at, length in pieces(slot * rows_here, rows_here, block):
                begin = z * rows_here + at
                place_at = (j, z) if k in in_a else (z, j)
                for h in range(2):
                    part[(h, *place_at, pl.ds(offset, length), slice(None))] = rounded[
                        begin : begin + length, h * half : (h + 1) * half
                    ]

    keep(
        9,
        lax.dot_general(
            slopes[...].reshape(groups * flat, channels),
            states_bf[...].reshape(groups * flat, state_width),
            (((0,), (0,)), ((), ())), preferred_element_type=F32
        ),
    )
    for part, slots, used, block in (
        (grads_a, slots_a, len(in_a), block_a),
        (grads_b, slots_b, len(in_b), block_b),
    ):
        if used < slots:
            for j, offset, _, length in pieces(
                used * rows_here, (slots - used) * rows_here, block
            ):
                for h in range(2):
                    for z in range(nz):
                        place_at = (j, z) if part is grads_a else (z, j)
                        part[(h, *place_at, pl.ds(offset, length), slice(None))] = jnp.zeros(
                            (length, half), BF16
                        )
    transpose_taps(4, 9)
    for copies in gd_copies:
        for copy in copies:
            copy.wait_recv()
    for g in range(groups):
        for f in range(frames_here):
            back = jnp.concatenate(
                [
                    gd_recv[g, s, f * part_cells : (f + 1) * part_cells, :].astype(F32)
                    for s in range(n)
                ],
                axis=0,
            ).astype(BF16)
            drive_flat[pl.ds((g * frames_here + f) * group_cells, group_cells), :] = back
            drive[f, g * group_rows : (g + 1) * group_rows] = back.reshape(
                group_rows, width, state_width
            )
    edge_start(drive, drive_halo, dhalo_ss, dhalo_rs)
    flat_drive = drive_flat[...]

    def tap_gradient(k):
        keep(
            k,
            jnp.dot(
                taps_t[pl.ds(k * channels, channels), :], flat_drive, preferred_element_type=F32
            ),
        )

    def over_pair(grads, pair, own, count, ss, rs):
        copies = []
        for d in list(range(1, count)) + [0]:
            at = lax.rem(own + d, count)
            copies.append(
                remote(
                    grads.at[1 - core, at], pair.at[at], ss.at[d], rs.at[d],
                    {"tm": me + 1 - 2 * core},
                )
            )
            copies[-1].start()
        return copies

    for k in range(9):
        if k in in_b:
            tap_gradient(k)
    pair_b_copies = over_pair(grads_b, pair_b, band, nz, pairb_ss, pairb_rs)
    pair_a_copies = [
        remote(
            grads_a.at[1 - core, j], pair_a.at[j], paira_ss.at[j], paira_rs.at[j],
            {"tm": me + 1 - 2 * core},
        )
        for j in range(chips)
    ]
    sent = 0
    for k in range(9):
        if k in in_a:
            tap_gradient(k)
            while (sent + 1) * block_a <= (in_a[k] + 1) * rows_here:
                pair_a_copies[sent].start()
                sent += 1
    for copy in pair_a_copies[sent:]:
        copy.start()

    def first_sum(arrive, grads, pair, own, count, send, recv, ss, rs, where, total):
        copies = []
        for d in range(1, count):
            at = lax.rem(own + d, count)
            arrive(d, at)
            send[d - 1] = (grads[core, at].astype(F32) + pair[at].astype(F32)).astype(BF16)
            copies.append(
                remote(send.at[d - 1], recv.at[d - 1], ss.at[d - 1], rs.at[d - 1], where(at))
            )
            copies[-1].start()
        arrive(0, own)
        total[...] = grads[core, own].astype(F32) + pair[own].astype(F32)
        return copies

    def to_chip(j):
        return {"tm": 2 * j + core}

    def to_band(z):
        return {"row": z}

    def arrive_a(d, at):
        remote(
            grads_a.at[1 - core, at], pair_a.at[at], paira_ss.at[at], paira_rs.at[at],
            {"tm": me + 1 - 2 * core},
        ).wait_recv()

    one_b = first_sum(
        lambda d, at: pair_b_copies[d - 1].wait_recv(), grads_b, pair_b, band, nz, send1_b, recv1_b, one_b_ss, one_b_rs,
        to_band, total_b,
    )
    one_a = first_sum(
        arrive_a, grads_a, pair_a, chip, chips, send1_a, recv1_a, one_a_ss, one_a_rs,
        to_chip, total_a,
    )

    for f in range(frames_here):
        for r in range(rows):
            place(drive_taps, row_at, f, r + 1, drive[f, r], rows, width)
    edge_wait(drive, drive_halo, dhalo_ss, dhalo_rs, True)
    for f in range(frames_here):
        place(drive_taps, row_at, f, 0, drive_halo[0, f], rows, width)
        place(drive_taps, row_at, f, rows + 1, drive_halo[1, f], rows, width)
    for g in range(groups):
        spread = jnp.concatenate(
            [
                feedthrough[...]
                * cotangent[f, g * group_cells : (g + 1) * group_cells, :].astype(F32)
                for f in range(frames_here)
            ],
            axis=0,
        )
        for k in range(9):
            spread = spread + lax.dot_general(
                drive_taps[in_group(g), pl.ds(k * state_width, state_width)],
                kernel[pl.ds((8 - k) * channels, channels), :],
                (((1,), (1,)), ((), ())),
                preferred_element_type=F32,
            )
        for f in range(frames_here):
            grad_frames[f, g * group_cells : (g + 1) * group_cells, :] = spread[
                f * group_cells : (f + 1) * group_cells
            ].astype(BF16)

    def second_sum(one, recv1, total, own, count, send, recv, ss, rs, where):
        summed = total[...]
        for i, copy in enumerate(one):
            copy.wait_recv()
            summed = summed + recv1[i].astype(F32)
        total[...] = summed
        send[...] = summed.astype(BF16)
        copies = []
        for d in range(1, count):
            at = lax.rem(own + d, count)
            copies.append(
                remote(send.at[at], recv.at[d - 1], ss.at[d - 1], rs.at[d - 1], where(at))
            )
            copies[-1].start()
        return copies

    two_b = second_sum(
        one_b, recv1_b, total_b, chip, chips, send2_b, recv2_b, two_b_ss, two_b_rs, to_chip
    )
    two_a = second_sum(
        one_a, recv1_a, total_a, band, nz, send2_a, recv2_a, two_a_ss, two_a_rs, to_band
    )
    for two, recv2, total, own, begin, block in (
        (two_b, recv2_b, total_b, chip, block_a, block_b),
        (two_a, recv2_a, total_a, band, 0, block_a),
    ):
        mine = total[own]
        for i, copy in enumerate(two):
            copy.wait_recv()
            mine = mine + recv2[i].astype(F32)
        final[me, pl.ds(begin, block), :] = mine.astype(BF16)

    sibling = {"tm": me + 1 - 2 * core}
    fin_copies = []
    for d in range(1, chips):
        j = lax.rem(chip + d, chips)
        fin_copies.append(
            remote(final.at[me], final.at[me], fin_ss.at[d - 1], fin_rs.at[d - 1], to_chip(j))
        )
    sib_copies = []
    for d in range(chips):
        at = 2 * lax.rem(chip - d + chips, chips) + core
        sib_copies.append(
            remote(final.at[at], final.at[at], sib_ss.at[d], sib_rs.at[d], sibling)
        )
    for copy in fin_copies:
        copy.start()
    sib_copies[0].start()
    flat_copies = dec_copies
    for copies in [cot_copies] + drv_copies + gd_copies:
        flat_copies = flat_copies + copies
    for copies in (pair_a_copies, pair_b_copies, one_a, one_b, two_a, two_b):
        flat_copies = flat_copies + copies
    for copy in flat_copies:
        copy.wait_send()
    edge_wait(frames_hbm, halo, halo_ss, halo_rs, False)
    edge_wait(drive, drive_halo, dhalo_ss, dhalo_rs, False)
    for d in range(1, chips):
        fin_copies[d - 1].wait_recv()
        sib_copies[d].start()
    for copy in sib_copies:
        copy.wait_recv()
    for copy in fin_copies + sib_copies:
        copy.wait_send()


def finish(
    dims,
    spread, final, grad_frames, grad_kernel, grad_readout,
    scaled, scaled_readout, sems,
):
    chips, slots_a, block_a, block_b, in_a, in_b, scaling = dims
    rows_here, state_width = scaled_readout.shape
    half = state_width // 2
    through = pltpu.make_async_copy(spread, grad_frames, sems.at[0])
    through.start()
    for k in range(10):
        slot, block, begin = (in_a[k], block_a, 0) if k in in_a else (in_b[k], block_b, block_a)
        for j, offset, at, length in pieces(slot * rows_here, rows_here, block):
            for h in range(2):
                value = final[2 * j + h, pl.ds(begin + offset, length), :].astype(F32) * scaling
                lanes = pl.ds(h * half, half)
                if k < 9:
                    scaled[k, pl.ds(at, length), lanes] = value
                else:
                    scaled_readout[pl.ds(at, length), lanes] = value
    stores = [
        pltpu.make_async_copy(scaled, grad_kernel, sems.at[1]),
        pltpu.make_async_copy(scaled_readout, grad_readout, sems.at[2]),
    ]
    for store in stores:
        store.start()
    for copy in stores + [through]:
        copy.wait()


def local(n, nz, frames_in, cotangent, kernel, readout, feedthrough, decay_rate, start_state):
    frames_here, rows, width, channels = frames_in.shape
    state_width = kernel.shape[2]
    cells = rows * width
    share = cells // n
    chips = n // 2
    rows_here = channels // nz
    half = state_width // 2
    step = 16 * chips // math.gcd(rows_here, 16 * chips)
    slots_a = -(-7 // step) * step
    slots_b = -(-max(10 - slots_a, 1) // step) * step
    block_a = slots_a * rows_here // chips
    block_b = slots_b * rows_here // chips
    groups = 2 if frames_here * share // 2 % 16 == 0 and share % 16 == 0 and rows % 2 == 0 else 1
    mixed = frames_here * share // groups
    scaling = 1.0 / math.sqrt(frames_here * cells * n * nz)
    vmem = pltpu.VMEM
    dma = pltpu.SemaphoreType.DMA
    any_space = pl.BlockSpec(memory_space=pl.ANY)
    whole = pl.BlockSpec(memory_space=pltpu.VMEM)
    hbm = pl.BlockSpec(memory_space=pltpu.HBM)
    every = frames_here * cells
    scratch = [
        vmem(frames_in.shape, BF16),
        vmem((frames_here, cells, channels), BF16),
        vmem((9 * channels, state_width), BF16),
        vmem(readout.shape, BF16),
        vmem((1, channels), F32),
        vmem(decay_rate.shape, F32),
        vmem((cells, state_width), F32),
        dma((7,)),
        vmem((every, 9 * channels), BF16),
        vmem((9 * channels, every), BF16),
                vmem((every, 9 * state_width), BF16),
        vmem((2, frames_here, width, channels), BF16),
        vmem((2, frames_here, width, state_width), BF16),
        vmem((8, state_width), F32),
        vmem((n, 8, state_width), F32),
        vmem((n, groups, mixed, channels), BF16),
        vmem((n, groups, mixed, channels), BF16),
        vmem((groups, frames_here, cells // groups, state_width), F32),
        vmem((groups, n, mixed, state_width), BF16),
        vmem((groups, n, mixed, state_width), BF16),
        vmem((groups, n, mixed, state_width), BF16),
        vmem((groups, n * mixed, channels), BF16),
        vmem((n * mixed, state_width), F32),
        vmem((groups, n, mixed, state_width), BF16),
        vmem((groups, n, mixed, state_width), BF16),
        vmem((frames_here, rows, width, state_width), BF16),
        vmem((every, state_width), BF16),
        vmem((2, chips, nz, block_a, half), BF16),
        vmem((2, nz, chips, block_b, half), BF16),
        vmem((chips, nz, block_a, half), BF16),
        vmem((nz, chips, block_b, half), BF16),
        vmem((chips - 1, nz, block_a, half), BF16),
        vmem((nz - 1, chips, block_b, half), BF16),
        vmem((chips - 1, nz, block_a, half), BF16),
        vmem((nz - 1, chips, block_b, half), BF16),
        vmem((nz, block_a, half), F32),
        vmem((chips, block_b, half), F32),
        vmem((nz, block_a, half), BF16),
        vmem((chips, block_b, half), BF16),
        vmem((nz - 1, block_a, half), BF16),
        vmem((chips - 1, block_b, half), BF16),
    ]
    counts = ((2,), (n - 1,), (n - 1,), (groups, n - 1), (groups, n - 1), (2,))
    counts += ((chips,), (nz,), (chips - 1,), (nz - 1,), (nz - 1,), (chips - 1,))
    for count in counts + ((chips - 1,), (chips,)):
        scratch += [dma(count), dma(count)]
    spread, gathered = pl.pallas_call(
        functools.partial(fused, (n, nz, slots_a, slots_b, groups)),
        out_shape=(
            vmem((frames_here, cells, channels), BF16),
            vmem((n, block_a + block_b, half), BF16),
        ),
        in_specs=[hbm] * 7,
        out_specs=(whole, whole),
        scratch_shapes=scratch,
        compiler_params=pltpu.CompilerParams(
            collective_id=0, has_side_effects=True, vmem_limit_bytes=48 * 1024 * 1024
        ),
        cost_estimate=pl.CostEstimate(
            flops=2 * every * channels * state_width * 30,
            bytes_accessed=6 * 1024 * 1024,
            transcendentals=every * channels,
        ),
        name="conv_s5_backward",
    )(
        *(
            pltpu.with_memory_space_constraint(argument, pltpu.HBM)
            for argument in (
                frames_in,
                cotangent.reshape(frames_here, cells, channels),
                kernel.reshape(9 * channels, state_width),
                readout,
                feedthrough.reshape(1, channels),
                decay_rate,
                start_state.reshape(cells, state_width),
            )
        )
    )
    in_a, in_b = places(slots_a)
    spread, kernel_part, readout_part = pl.pallas_call(
        functools.partial(finish, (chips, slots_a, block_a, block_b, in_a, in_b, scaling)),
        out_shape=(
            jax.ShapeDtypeStruct((frames_here, cells, channels), BF16),
            jax.ShapeDtypeStruct((9, rows_here, state_width), F32),
            jax.ShapeDtypeStruct((rows_here, state_width), F32),
        ),
        in_specs=[whole] * 2,
        out_specs=(any_space,) * 3,
        scratch_shapes=[
            vmem((9, rows_here, state_width), F32),
            vmem((rows_here, state_width), F32),
            dma((3,)),
        ],
        compiler_params=pltpu.CompilerParams(vmem_limit_bytes=48 * 1024 * 1024),
        name="write_outputs",
    )(spread, gathered)
    return (spread.reshape(frames_in.shape), kernel_part, readout_part.T)


def solution(mesh):
    placed = (
        P("tm", "row", None, None),
        P("tm", "row", None, None),
        P(),
        P(),
        P(),
        P("tm", None),
        P("row", None, None),
    )
    return jax.shard_map(
        functools.partial(local, mesh.shape["tm"], mesh.shape["row"]),
        mesh=mesh,
        in_specs=placed,
        out_specs=(P("tm", "row", None, None), P(None, "row", None), P(None, "row")),
        check_vma=False,
    )
```

```python
import functools
import math

import jax
import jax.numpy as jnp
from jax import lax
from jax.experimental import pallas as pl
from jax.experimental.pallas import tpu as pltpu
from jax.sharding import PartitionSpec as P

SQRT_TWO_PI = 0.7978845608
CUBIC = 0.044715
F32 = jnp.float32
BF16 = jnp.bfloat16
MESH = pl.DeviceIdType.MESH


def gelu_slope(mixture):
    square = mixture * mixture
    tangent = jnp.tanh(SQRT_TWO_PI * (mixture + CUBIC * square * mixture))
    return 0.5 * (1.0 + tangent) + 0.5 * mixture * (1.0 - tangent * tangent) * SQRT_TWO_PI * (
        1.0 + 3.0 * CUBIC * square
    )


def place(taps, row_at, frame, padded_row, cells, rows, width):
    channels = cells.shape[1]
    wide = cells.astype(F32)
    column = lax.broadcasted_iota(jnp.int32, wide.shape, 0)
    before = jnp.where(column == 0, 0.0, pltpu.roll(wide, 1, 0)).astype(BF16)
    after = jnp.where(column == width - 1, 0.0, pltpu.roll(wide, width - 1, 0)).astype(BF16)
    for j, shifted in enumerate((before, cells, after)):
        for i in range(3):
            h = padded_row - i
            if 0 <= h < rows:
                k = 3 * i + j
                taps[
                    pl.ds(row_at(frame, h), width), pl.ds(k * channels, channels)
                ] = shifted


def pieces(start, size, block):
    done = 0
    while done < size:
        at = start + done
        length = min(size - done, block - at % block)
        yield at // block, at % block, done, length
        done += length


def places(slots_a):
    taps_a = min(slots_a, 9)
    in_a = {k: i for i, k in enumerate(range(9 - taps_a, 9))}
    in_b = {k: i for i, k in enumerate([9] + list(range(9 - taps_a)))}
    return in_a, in_b


def fused(
    dims,
    frames_hbm, cotangent_hbm, kernel_hbm, readout_hbm, feedthrough_hbm, decay_hbm, start_hbm,
    grad_frames, final,
    frames, cotangent, kernel, readout, feedthrough, decay, start_state, load_sems,
    taps, taps_t, drive_taps,
    halo, drive_halo, own_decay, all_decay,
    cot_send, cot_recv, driven, drv_send, drv_recv,
    states_bf, slopes, pulled, gd_send, gd_recv, drive, drive_flat,
    grads_a, grads_b, pair_a, pair_b, send1_a, send1_b, recv1_a, recv1_b, total_a, total_b,
    send2_a, send2_b, recv2_a, recv2_b,
    halo_ss, halo_rs, dec_ss, dec_rs, cot_ss, cot_rs, drv_ss, drv_rs, gd_ss, gd_rs,
    dhalo_ss, dhalo_rs, paira_ss, paira_rs, pairb_ss, pairb_rs, one_a_ss, one_a_rs,
    one_b_ss, one_b_rs, two_a_ss, two_a_rs, two_b_ss, two_b_rs, fin_ss, fin_rs, sib_ss, sib_rs,
):
    n, nz, slots_a, slots_b, groups = dims
    loads = [
        pltpu.make_async_copy(src, dst, load_sems.at[i])
        for i, (src, dst) in enumerate(
            (
                (decay_hbm, decay), (frames_hbm, frames), (cotangent_hbm, cotangent),
                (kernel_hbm, kernel), (start_hbm, start_state), (readout_hbm, readout),
                (feedthrough_hbm, feedthrough),
            )
        )
    ]
    for load in loads:
        load.start()
    frames_here, rows, width, channels = frames.shape
    state_width = kernel.shape[1]
    band_cells = rows * width
    share = band_cells // n
    chips = n // 2
    part_cells = share // groups
    half = state_width // 2
    me = lax.axis_index("tm")
    band = lax.axis_index("row")
    core = lax.rem(me, 2)
    chip = lax.div(me, 2)

    def remote(src, dst, send_sem, recv_sem, where):
        return pltpu.make_async_remote_copy(
            src_ref=src, dst_ref=dst, send_sem=send_sem, recv_sem=recv_sem,
            device_id=where, device_id_type=MESH,
        )

    barrier = pltpu.get_barrier_semaphore()
    for d in range(1, n):
        pl.semaphore_signal(
            barrier, inc=1, device_id={"tm": lax.rem(me + d, n)}, device_id_type=MESH
        )
    for d in range(1, nz):
        pl.semaphore_signal(
            barrier, inc=1, device_id={"row": lax.rem(band + d, nz)}, device_id_type=MESH
        )

    own_decay[...] = jnp.zeros_like(own_decay)
    loads[0].wait()
    own_decay[0:frames_here, :] = decay[...]
    all_decay[me] = own_decay[...]
    pl.semaphore_wait(barrier, (n - 1) + (nz - 1))

    def edge_copies(src, dst, ss, rs):
        up = remote(src.at[:, 0], dst.at[1], ss.at[0], rs.at[1], {"row": band - 1})
        down = remote(src.at[:, rows - 1], dst.at[0], ss.at[1], rs.at[0], {"row": band + 1})
        return up, down

    def edge_start(src, dst, ss, rs):
        up, down = edge_copies(src, dst, ss, rs)

        @pl.when(band > 0)
        def _():
            up.start()

        @pl.when(band < nz - 1)
        def _():
            down.start()

        @pl.when(band == 0)
        def _():
            dst[0] = jnp.zeros(dst.shape[1:], BF16)

        @pl.when(band == nz - 1)
        def _():
            dst[1] = jnp.zeros(dst.shape[1:], BF16)

    def edge_wait(src, dst, ss, rs, arrived):
        up, down = edge_copies(src, dst, ss, rs)

        @pl.when(band > 0)
        def _():
            if arrived:
                down.wait_recv()
            else:
                up.wait_send()

        @pl.when(band < nz - 1)
        def _():
            if arrived:
                up.wait_recv()
            else:
                down.wait_send()

    edge_start(frames_hbm, halo, halo_ss, halo_rs)
    loads[1].wait()
    def over_tm(src_of, dst, ss, rs):
        copies = []
        for d in range(1, n):
            to = lax.rem(me + d, n)
            copies.append(
                remote(src_of(to), dst.at[me], ss.at[d - 1], rs.at[d - 1], {"tm": to})
            )
        return copies

    group_cells = band_cells // groups
    group_rows = rows // groups

    def cells_of(s, g):
        begin = g * group_cells + s * part_cells
        return slice(begin, begin + part_cells)

    def row_at(f, h):
        return ((h // group_rows * frames_here + f) * group_rows + h % group_rows) * width

    def in_group(g):
        return pl.ds(g * frames_here * group_cells, frames_here * group_cells)


    dec_copies = over_tm(lambda to: own_decay, all_decay, dec_ss, dec_rs)
    for copy in dec_copies:
        copy.start()
    for f in range(frames_here):
        for r in range(rows):
            place(taps, row_at, f, r + 1, frames[f, r], rows, width)
    loads[2].wait()
    for s in range(n):
        for g in range(groups):
            cot_send[s, g] = jnp.concatenate(
                [cotangent[f, cells_of(s, g), :] for f in range(frames_here)], axis=0
            )
    cot_copies = over_tm(lambda to: cot_send.at[to], cot_recv, cot_ss, cot_rs)
    for copy in cot_copies:
        copy.start()
    cot_recv[me] = cot_send[me]
    rim_taps = ((0, 0, pl.ds(0, 3 * channels)), (1, rows - 1, pl.ds(6 * channels, 3 * channels)))
    for _, h, columns in rim_taps:
        for f in range(frames_here):
            taps[pl.ds(row_at(f, h), width), columns] = jnp.zeros((width, 3 * channels), BF16)
    loads[3].wait()
    for g in range(groups):
        driven[g] = jnp.dot(
            taps[in_group(g), :], kernel[...], preferred_element_type=F32
        ).reshape(driven.shape[1:])
    edge_wait(frames_hbm, halo, halo_ss, halo_rs, True)
    for f in range(frames_here):
        place(taps, row_at, f, 0, halo[0, f], rows, width)
        place(taps, row_at, f, rows + 1, halo[1, f], rows, width)
    drv_copies = []
    for g in range(groups):
        for _, h, columns in rim_taps:
            if h // group_rows == g:
                rim = jnp.concatenate(
                    [taps[pl.ds(row_at(f, h), width), columns] for f in range(frames_here)], axis=0
                )
                added = jnp.dot(rim, kernel[columns, :], preferred_element_type=F32)
                at = pl.ds(h % group_rows * width, width)
                for f in range(frames_here):
                    driven[g, f, at, :] += added[f * width : (f + 1) * width]
        for s in range(n):
            drv_send[g, s] = jnp.concatenate(
                [
                    driven[g, f, s * part_cells : (s + 1) * part_cells, :]
                    for f in range(frames_here)
                ],
                axis=0,
            ).astype(BF16)
        drv_copies.append(
            over_tm(
                lambda to, g=g: drv_send.at[g, to], drv_recv.at[g], drv_ss.at[g], drv_rs.at[g]
            )
        )
        for copy in drv_copies[g]:
            copy.start()
        drv_recv[g, me] = drv_send[g, me]

    def transpose_taps(first, last):
        for k in range(first, last):
            taps_t[pl.ds(k * channels, channels), :] = taps[:, pl.ds(k * channels, channels)].T

    transpose_taps(0, 4)
    for load in loads[4:7]:
        load.wait()

    for copy in dec_copies:
        copy.wait_recv()
    flat = n * frames_here * part_cells
    gd_copies = []
    for g in range(groups):
        for copy in drv_copies[g]:
            copy.wait_recv()
        begin = pl.multiple_of(g * group_cells + me * part_cells, part_cells)
        state = start_state[pl.ds(begin, part_cells), :]
        for s in range(n):
            arrived = drv_recv[g, s].astype(F32)
            kept = []
            for f in range(frames_here):
                rate = all_decay[s, f : f + 1, :]
                gain = jnp.sqrt(1.0 - rate * rate)
                state = rate * state + gain * arrived[f * part_cells : (f + 1) * part_cells]
                kept.append(state)
            states_bf[g, s] = jnp.concatenate(kept, axis=0).astype(BF16)
        if g == 0:
            for copy in cot_copies:
                copy.wait_recv()
        mixture = jnp.dot(
            states_bf[g].reshape(flat, state_width), readout[...], preferred_element_type=F32
        )
        slopes[g] = (
            cot_recv[:, g].reshape(flat, channels).astype(F32) * gelu_slope(mixture)
        ).astype(BF16)
        pulled[...] = lax.dot_general(
            slopes[g], readout[...], (((1,), (1,)), ((), ())), preferred_element_type=F32
        )
        adjoint = jnp.zeros((part_cells, state_width), F32)
        rate = jnp.zeros((1, state_width), F32)
        for s in reversed(range(n)):
            kept = []
            for f in reversed(range(frames_here)):
                at = (s * frames_here + f) * part_cells
                adjoint = pulled[at : at + part_cells, :] + rate * adjoint
                rate = all_decay[s, f : f + 1, :]
                kept.append(jnp.sqrt(1.0 - rate * rate) * adjoint)
            gd_send[g, s] = jnp.concatenate(kept[::-1], axis=0).astype(BF16)
        gd_copies.append(
            over_tm(lambda to, g=g: gd_send.at[g, to], gd_recv.at[g], gd_ss.at[g], gd_rs.at[g])
        )
        for copy in gd_copies[g]:
            copy.start()
        gd_recv[g, me] = gd_send[g, me]

    rows_here = channels // nz
    block_a = slots_a * rows_here // chips
    block_b = slots_b * rows_here // chips
    in_a, in_b = places(slots_a)

    def keep(k, product):
        rounded = product.astype(BF16)
        part, slot, block = (
            (grads_a, in_a[k], block_a) if k in in_a else (grads_b, in_b[k], block_b)
        )
        for z in range(nz):
            for j, offset, at, length in pieces(slot * rows_here, rows_here, block):
                begin = z * rows_here + at
                place_at = (j, z) if k in in_a else (z, j)
                for h in range(2):
                    part[(h, *place_at, pl.ds(offset, length), slice(None))] = rounded[
                        begin : begin + length, h * half : (h + 1) * half
                    ]

    keep(
        9,
        lax.dot_general(
            slopes[...].reshape(groups * flat, channels),
            states_bf[...].reshape(groups * flat, state_width),
            (((0,), (0,)), ((), ())), preferred_element_type=F32
        ),
    )
    for part, slots, used, block in (
        (grads_a, slots_a, len(in_a), block_a),
        (grads_b, slots_b, len(in_b), block_b),
    ):
        if used < slots:
            for j, offset, _, length in pieces(
                used * rows_here, (slots - used) * rows_here, block
            ):
                for h in range(2):
                    for z in range(nz):
                        place_at = (j, z) if part is grads_a else (z, j)
                        part[(h, *place_at, pl.ds(offset, length), slice(None))] = jnp.zeros(
                            (length, half), BF16
                        )
    transpose_taps(4, 9)
    for copies in gd_copies:
        for copy in copies:
            copy.wait_recv()
    for g in range(groups):
        for f in range(frames_here):
            back = jnp.concatenate(
                [
                    gd_recv[g, s, f * part_cells : (f + 1) * part_cells, :].astype(F32)
                    for s in range(n)
                ],
                axis=0,
            ).astype(BF16)
            drive_flat[pl.ds((g * frames_here + f) * group_cells, group_cells), :] = back
            drive[f, g * group_rows : (g + 1) * group_rows] = back.reshape(
                group_rows, width, state_width
            )
    edge_start(drive, drive_halo, dhalo_ss, dhalo_rs)
    flat_drive = drive_flat[...]

    def tap_gradient(k):
        keep(
            k,
            jnp.dot(
                taps_t[pl.ds(k * channels, channels), :], flat_drive, preferred_element_type=F32
            ),
        )

    def over_pair(grads, pair, own, count, ss, rs):
        copies = []
        for d in list(range(1, count)) + [0]:
            at = lax.rem(own + d, count)
            copies.append(
                remote(
                    grads.at[1 - core, at], pair.at[at], ss.at[d], rs.at[d],
                    {"tm": me + 1 - 2 * core},
                )
            )
            copies[-1].start()
        return copies

    for k in range(9):
        if k in in_b:
            tap_gradient(k)
    pair_b_copies = over_pair(grads_b, pair_b, band, nz, pairb_ss, pairb_rs)
    pair_a_copies = [
        remote(
            grads_a.at[1 - core, j], pair_a.at[j], paira_ss.at[j], paira_rs.at[j],
            {"tm": me + 1 - 2 * core},
        )
        for j in range(chips)
    ]
    def first_sum(arrive, grads, pair, own, count, send, recv, ss, rs, where, total):
        copies = []
        for d in range(1, count):
            at = lax.rem(own + d, count)
            arrive(d, at)
            send[d - 1] = (grads[core, at].astype(F32) + pair[at].astype(F32)).astype(BF16)
            copies.append(
                remote(send.at[d - 1], recv.at[d - 1], ss.at[d - 1], rs.at[d - 1], where(at))
            )
            copies[-1].start()
        arrive(0, own)
        total[...] = grads[core, own].astype(F32) + pair[own].astype(F32)
        return copies

    def to_chip(j):
        return {"tm": 2 * j + core}

    def to_band(z):
        return {"row": z}

    def arrive_a(d, at):
        remote(
            grads_a.at[1 - core, at], pair_a.at[at], paira_ss.at[at], paira_rs.at[at],
            {"tm": me + 1 - 2 * core},
        ).wait_recv()

    early = min(3, len(in_a)) - 1
    sent = 0
    for k in range(9):
        if k in in_a:
            tap_gradient(k)
            while (sent + 1) * block_a <= (in_a[k] + 1) * rows_here:
                pair_a_copies[sent].start()
                sent += 1
            if in_a[k] == early:
                one_b = first_sum(
                    lambda d, at: pair_b_copies[d - 1].wait_recv(),
                    grads_b, pair_b, band, nz, send1_b, recv1_b, one_b_ss, one_b_rs,
                    to_band, total_b,
                )
    for copy in pair_a_copies[sent:]:
        copy.start()
    one_a = first_sum(
        arrive_a, grads_a, pair_a, chip, chips, send1_a, recv1_a, one_a_ss, one_a_rs,
        to_chip, total_a,
    )

    for f in range(frames_here):
        for r in range(rows):
            place(drive_taps, row_at, f, r + 1, drive[f, r], rows, width)
    edge_wait(drive, drive_halo, dhalo_ss, dhalo_rs, True)
    for f in range(frames_here):
        place(drive_taps, row_at, f, 0, drive_halo[0, f], rows, width)
        place(drive_taps, row_at, f, rows + 1, drive_halo[1, f], rows, width)
    for g in range(groups):
        spread = jnp.concatenate(
            [
                feedthrough[...]
                * cotangent[f, g * group_cells : (g + 1) * group_cells, :].astype(F32)
                for f in range(frames_here)
            ],
            axis=0,
        )
        for k in range(9):
            spread = spread + lax.dot_general(
                drive_taps[in_group(g), pl.ds(k * state_width, state_width)],
                kernel[pl.ds((8 - k) * channels, channels), :],
                (((1,), (1,)), ((), ())),
                preferred_element_type=F32,
            )
        for f in range(frames_here):
            grad_frames[f, g * group_cells : (g + 1) * group_cells, :] = spread[
                f * group_cells : (f + 1) * group_cells
            ].astype(BF16)

    def second_sum(one, recv1, total, own, count, send, recv, ss, rs, where):
        summed = total[...]
        for i, copy in enumerate(one):
            copy.wait_recv()
            summed = summed + recv1[i].astype(F32)
        total[...] = summed
        send[...] = summed.astype(BF16)
        copies = []
        for d in range(1, count):
            at = lax.rem(own + d, count)
            copies.append(
                remote(send.at[at], recv.at[d - 1], ss.at[d - 1], rs.at[d - 1], where(at))
            )
            copies[-1].start()
        return copies

    two_b = second_sum(
        one_b, recv1_b, total_b, chip, chips, send2_b, recv2_b, two_b_ss, two_b_rs, to_chip
    )
    two_a = second_sum(
        one_a, recv1_a, total_a, band, nz, send2_a, recv2_a, two_a_ss, two_a_rs, to_band
    )
    for two, recv2, total, own, begin, block in (
        (two_b, recv2_b, total_b, chip, block_a, block_b),
        (two_a, recv2_a, total_a, band, 0, block_a),
    ):
        mine = total[own]
        for i, copy in enumerate(two):
            copy.wait_recv()
            mine = mine + recv2[i].astype(F32)
        final[me, pl.ds(begin, block), :] = mine.astype(BF16)

    sibling = {"tm": me + 1 - 2 * core}
    fin_copies = []
    for d in range(1, chips):
        j = lax.rem(chip + d, chips)
        fin_copies.append(
            remote(final.at[me], final.at[me], fin_ss.at[d - 1], fin_rs.at[d - 1], to_chip(j))
        )
    sib_copies = []
    for d in range(chips):
        at = 2 * lax.rem(chip - d + chips, chips) + core
        sib_copies.append(
            remote(final.at[at], final.at[at], sib_ss.at[d], sib_rs.at[d], sibling)
        )
    for copy in fin_copies:
        copy.start()
    sib_copies[0].start()
    flat_copies = dec_copies
    for copies in [cot_copies] + drv_copies + gd_copies:
        flat_copies = flat_copies + copies
    for copies in (pair_a_copies, pair_b_copies, one_a, one_b, two_a, two_b):
        flat_copies = flat_copies + copies
    for copy in flat_copies:
        copy.wait_send()
    edge_wait(frames_hbm, halo, halo_ss, halo_rs, False)
    edge_wait(drive, drive_halo, dhalo_ss, dhalo_rs, False)
    for d in range(1, chips):
        fin_copies[d - 1].wait_recv()
        sib_copies[d].start()
    for copy in sib_copies:
        copy.wait_recv()
    for copy in fin_copies + sib_copies:
        copy.wait_send()


def finish(
    dims,
    spread, final, grad_frames, grad_kernel, grad_readout,
    scaled, scaled_readout, sems,
):
    chips, slots_a, block_a, block_b, in_a, in_b, scaling = dims
    rows_here, state_width = scaled_readout.shape
    half = state_width // 2
    through = pltpu.make_async_copy(spread, grad_frames, sems.at[0])
    through.start()
    for k in range(10):
        slot, block, begin = (in_a[k], block_a, 0) if k in in_a else (in_b[k], block_b, block_a)
        for j, offset, at, length in pieces(slot * rows_here, rows_here, block):
            for h in range(2):
                value = final[2 * j + h, pl.ds(begin + offset, length), :].astype(F32) * scaling
                lanes = pl.ds(h * half, half)
                if k < 9:
                    scaled[k, pl.ds(at, length), lanes] = value
                else:
                    scaled_readout[pl.ds(at, length), lanes] = value
    stores = [
        pltpu.make_async_copy(scaled, grad_kernel, sems.at[1]),
        pltpu.make_async_copy(scaled_readout, grad_readout, sems.at[2]),
    ]
    for store in stores:
        store.start()
    for copy in stores + [through]:
        copy.wait()


def local(n, nz, frames_in, cotangent, kernel, readout, feedthrough, decay_rate, start_state):
    frames_here, rows, width, channels = frames_in.shape
    state_width = kernel.shape[2]
    cells = rows * width
    share = cells // n
    chips = n // 2
    rows_here = channels // nz
    half = state_width // 2
    step = 16 * chips // math.gcd(rows_here, 16 * chips)
    slots_a = -(-6 // step) * step
    slots_b = -(-max(10 - slots_a, 1) // step) * step
    block_a = slots_a * rows_here // chips
    block_b = slots_b * rows_here // chips
    groups = 2 if frames_here * share // 2 % 16 == 0 and share % 16 == 0 and rows % 2 == 0 else 1
    mixed = frames_here * share // groups
    scaling = 1.0 / math.sqrt(frames_here * cells * n * nz)
    vmem = pltpu.VMEM
    dma = pltpu.SemaphoreType.DMA
    any_space = pl.BlockSpec(memory_space=pl.ANY)
    whole = pl.BlockSpec(memory_space=pltpu.VMEM)
    hbm = pl.BlockSpec(memory_space=pltpu.HBM)
    every = frames_here * cells
    scratch = [
        vmem(frames_in.shape, BF16),
        vmem((frames_here, cells, channels), BF16),
        vmem((9 * channels, state_width), BF16),
        vmem(readout.shape, BF16),
        vmem((1, channels), F32),
        vmem(decay_rate.shape, F32),
        vmem((cells, state_width), F32),
        dma((7,)),
        vmem((every, 9 * channels), BF16),
        vmem((9 * channels, every), BF16),
                vmem((every, 9 * state_width), BF16),
        vmem((2, frames_here, width, channels), BF16),
        vmem((2, frames_here, width, state_width), BF16),
        vmem((8, state_width), F32),
        vmem((n, 8, state_width), F32),
        vmem((n, groups, mixed, channels), BF16),
        vmem((n, groups, mixed, channels), BF16),
        vmem((groups, frames_here, cells // groups, state_width), F32),
        vmem((groups, n, mixed, state_width), BF16),
        vmem((groups, n, mixed, state_width), BF16),
        vmem((groups, n, mixed, state_width), BF16),
        vmem((groups, n * mixed, channels), BF16),
        vmem((n * mixed, state_width), F32),
        vmem((groups, n, mixed, state_width), BF16),
        vmem((groups, n, mixed, state_width), BF16),
        vmem((frames_here, rows, width, state_width), BF16),
        vmem((every, state_width), BF16),
        vmem((2, chips, nz, block_a, half), BF16),
        vmem((2, nz, chips, block_b, half), BF16),
        vmem((chips, nz, block_a, half), BF16),
        vmem((nz, chips, block_b, half), BF16),
        vmem((chips - 1, nz, block_a, half), BF16),
        vmem((nz - 1, chips, block_b, half), BF16),
        vmem((chips - 1, nz, block_a, half), BF16),
        vmem((nz - 1, chips, block_b, half), BF16),
        vmem((nz, block_a, half), F32),
        vmem((chips, block_b, half), F32),
        vmem((nz, block_a, half), BF16),
        vmem((chips, block_b, half), BF16),
        vmem((nz - 1, block_a, half), BF16),
        vmem((chips - 1, block_b, half), BF16),
    ]
    counts = ((2,), (n - 1,), (n - 1,), (groups, n - 1), (groups, n - 1), (2,))
    counts += ((chips,), (nz,), (chips - 1,), (nz - 1,), (nz - 1,), (chips - 1,))
    for count in counts + ((chips - 1,), (chips,)):
        scratch += [dma(count), dma(count)]
    spread, gathered = pl.pallas_call(
        functools.partial(fused, (n, nz, slots_a, slots_b, groups)),
        out_shape=(
            vmem((frames_here, cells, channels), BF16),
            vmem((n, block_a + block_b, half), BF16),
        ),
        in_specs=[hbm] * 7,
        out_specs=(whole, whole),
        scratch_shapes=scratch,
        compiler_params=pltpu.CompilerParams(
            collective_id=0, has_side_effects=True, vmem_limit_bytes=48 * 1024 * 1024
        ),
        cost_estimate=pl.CostEstimate(
            flops=2 * every * channels * state_width * 30,
            bytes_accessed=6 * 1024 * 1024,
            transcendentals=every * channels,
        ),
        name="conv_s5_backward",
    )(
        *(
            pltpu.with_memory_space_constraint(argument, pltpu.HBM)
            for argument in (
                frames_in,
                cotangent.reshape(frames_here, cells, channels),
                kernel.reshape(9 * channels, state_width),
                readout,
                feedthrough.reshape(1, channels),
                decay_rate,
                start_state.reshape(cells, state_width),
            )
        )
    )
    in_a, in_b = places(slots_a)
    spread, kernel_part, readout_part = pl.pallas_call(
        functools.partial(finish, (chips, slots_a, block_a, block_b, in_a, in_b, scaling)),
        out_shape=(
            jax.ShapeDtypeStruct((frames_here, cells, channels), BF16),
            jax.ShapeDtypeStruct((9, rows_here, state_width), F32),
            jax.ShapeDtypeStruct((rows_here, state_width), F32),
        ),
        in_specs=[whole] * 2,
        out_specs=(any_space,) * 3,
        scratch_shapes=[
            vmem((9, rows_here, state_width), F32),
            vmem((rows_here, state_width), F32),
            dma((3,)),
        ],
        compiler_params=pltpu.CompilerParams(vmem_limit_bytes=48 * 1024 * 1024),
        name="write_outputs",
    )(spread, gathered)
    return (spread.reshape(frames_in.shape), kernel_part, readout_part.T)


def solution(mesh):
    placed = (
        P("tm", "row", None, None),
        P("tm", "row", None, None),
        P(),
        P(),
        P(),
        P("tm", None),
        P("row", None, None),
    )
    return jax.shard_map(
        functools.partial(local, mesh.shape["tm"], mesh.shape["row"]),
        mesh=mesh,
        in_specs=placed,
        out_specs=(P("tm", "row", None, None), P(None, "row", None), P(None, "row")),
        check_vma=False,
    )
```
